32 devices in a mesh: dp: 4 (over y, x), seq: 8 (over z, core).
Axes of the slice: x: 2, y: 2, z: 4, core: 2. Of those that a mesh axis runs over, the one named last changes fastest.
Arguments:
- queries: bfloat16 [4, 1024, 4096], P('dp', 'seq'), may hold values from -6 to 6
- keys: bfloat16 [4, 1024, 512], P('dp', 'seq'), may hold values from -6 to 6
- values: bfloat16 [4, 1024, 512], P('dp', 'seq'), may hold values from -6 to 6
- grad_out: bfloat16 [4, 1024, 4096], P('dp', 'seq'), may hold values from -15 to 15
- layer_input: bfloat16 [4, 1024, 4096], P('dp', 'seq'), may hold values from -6 to 6
- basis_store: bfloat16 [4, 1024, 256], P('dp'), may hold values from -0.1875 to 0.1875
- owner: int32 [8], replicated, may hold values from 0 to 3
- layout: int32 [32, 8, 4], replicated, may hold values from -1 to 7, as said below
Outputs:
- grad_query: bfloat16 [4, 1024, 4096], P('dp', 'seq')
- lowrank_grad: float32 [4096, 256], P('seq')
The draws below stay inside these ranges and needn't reach their ends.
Inputs may be any that keep to these rules, and one draw needn't show every extreme that they name: layout[h, i] lists, in rising order, distinct key blocks from 0 to i, among them i itself, and then -1 in its unused slots; some list fills all 4 slots.
All inputs are finite; a program needn't handle non-finite values.
Results may differ from the reference program's by a relative error of at most 0.0088.
Values may be sent and summed in bfloat16 or wider, within the bound.
No kernel may reach another device: no remote copies, remote signals or barrier semaphores. Data moves between devices by JAX's collectives and lax.ppermute only.
A program may use at most 64 MiB of HBM per device.

```python
import jax
import jax.numpy as jnp
from jax import lax

HEADS = 32
KV_HEADS = 4
HEAD_DIM = 128
FEATURES = 4096
RANK = 256
BLOCK = 128
BATCH = 4
SEQ_LEN = 1024
HEAD_DEV = 4
GROUP = 8
KV_COLS = 512
NQB = 8
MAXSEL = 4


def draw_queries(key, part):
    shape = (BATCH, SEQ_LEN, HEADS, HEAD_DIM)
    draw_key = jax.random.fold_in(key, 11)
    base = jnp.clip(jax.random.normal(draw_key, shape, jnp.float32), -6.0, 6.0)
    return base.reshape(BATCH, SEQ_LEN, HEADS * HEAD_DIM).astype(jnp.bfloat16)


def draw_keys(key, part):
    shape = (BATCH, SEQ_LEN, KV_HEADS, HEAD_DIM)
    draw_key = jax.random.fold_in(key, 12)
    base = jnp.clip(jax.random.normal(draw_key, shape, jnp.float32), -6.0, 6.0)
    return base.reshape(BATCH, SEQ_LEN, KV_HEADS * HEAD_DIM).astype(jnp.bfloat16)


def draw_layout(key, part):
    base_key = jax.random.fold_in(key, 3)
    key_local, key_stride, key_phase, key_chosen = jax.random.split(base_key, 4)
    local_width = jax.random.randint(key_local, (HEADS,), 1, 4)
    stride = jax.random.randint(key_stride, (HEADS,), 8, 17)
    phase = jax.random.randint(key_phase, (HEADS,), 0, 1 << 20) % stride
    chosen = jax.random.randint(key_chosen, (), 0, HEADS)
    is_chosen = jnp.arange(HEADS, dtype=jnp.int32) == chosen
    local_width = jnp.where(is_chosen, 3, local_width)
    stride = jnp.where(is_chosen, 8, stride)
    phase = jnp.where(is_chosen, 0, phase)
    query_block = jnp.arange(NQB, dtype=jnp.int32)[None, :, None]
    key_block = jnp.arange(NQB, dtype=jnp.int32)[None, None, :]
    near = key_block > query_block - local_width[:, None, None]
    strided = key_block % stride[:, None, None] == phase[:, None, None]
    selected = (key_block <= query_block) & (near | strided)
    rank_in = jnp.cumsum(selected.astype(jnp.int32), axis=2) - 1
    slot_ids = jnp.arange(MAXSEL, dtype=jnp.int32)[:, None]
    hit = selected[:, :, None, :] & (rank_in[:, :, None, :] == slot_ids[None, None, :, :])
    listed = jnp.sum(hit.astype(jnp.int32) * jnp.arange(NQB, dtype=jnp.int32)[None, None, None, :], axis=3)
    present = jnp.any(hit, axis=3)
    return jnp.where(present, listed, -1).astype(jnp.int32)


def place_ends(result, rng, low, largest):
    spot = [jax.random.randint(jax.random.fold_in(rng, axis), (), 0, length) for axis, length in enumerate(result.shape)]
    longest = result.shape.index(max(result.shape))
    neighbour = spot[:longest] + [(spot[longest] + 1) % result.shape[longest]] + spot[longest + 1:]
    return result.at[tuple(spot)].set(low).at[tuple(neighbour)].set(largest)


def spiked(drawn, own_key, source, target, shards_of, factor):
    owner, partner = [(jnp.arange(drawn.shape[dim]) // (drawn.shape[dim] // shards_of)).reshape([-1 if axis == dim else 1 for axis in range(drawn.ndim)]) for dim in (source, target)]
    chosen = jax.random.permutation(own_key, shards_of)[partner]
    strong = (owner == chosen) | (owner == (partner + shards_of // 2) % shards_of)
    return jnp.where(strong, factor * drawn, drawn)


def levels(stream_key, extent, cuts, smallest, top_value):
    level = 1.0
    for axis_at, shards_of in cuts:
        heights = jax.random.uniform(jax.random.fold_in(jax.random.fold_in(stream_key, 6), axis_at), (shards_of,), jnp.float32, smallest / len(cuts), top_value / len(cuts))
        level = level * jnp.repeat(jnp.exp(heights), extent[axis_at] // shards_of).reshape((-1,) + (1,) * (len(extent) - 1 - axis_at))
    return level


def normal_values(rng, extent, scale, most, cuts=(), kind=jnp.bfloat16):
    values = jax.random.normal(rng, extent, jnp.float32) * scale
    if len(cuts) > 0:
        values = levels(rng, extent, cuts, -0.22, 0.18) * values
    return jnp.clip(values, min=-most, max=most).astype(kind)


def heavy_noise(stream_key, extent, width, most, cuts, heavy, kind=jnp.bfloat16):
    values = width * jax.random.normal(stream_key, extent, jnp.float32)
    if cuts:
        values = values * levels(stream_key, extent, cuts, -0.22, 0.18)
    return jnp.clip(spiked(values, jax.random.fold_in(stream_key, 3), *heavy), -most, most).astype(kind)


def setup_inputs(seed: int = 0) -> dict:
    seeds = jax.random.split(jax.random.key(seed), 9)
    queries = draw_queries(jax.random.fold_in(seeds[8], 71), 0)
    keys = draw_keys(jax.random.fold_in(seeds[8], 71), 0)
    values = normal_values(seeds[2], (BATCH, SEQ_LEN, KV_COLS), 1.0, 6.0, ((0, 4), (1, 8)))
    grad_out = normal_values(seeds[3], (BATCH, SEQ_LEN, HEADS * HEAD_DIM), 3.0, 15.0, ((0, 4), (1, 8)))
    layer_input = heavy_noise(seeds[4], (BATCH, SEQ_LEN, FEATURES), 1.0, 6.0, ((0, 4), (1, 8)), (1, 2, 8, 2.0))
    basis_store = normal_values(seeds[5], (BATCH, 2 * KV_COLS, RANK), (2 * KV_COLS) ** -0.5, 0.1875, ((0, 4),))
    owner = place_ends(jax.random.randint(seeds[6], (2 * KV_HEADS,), 0, BATCH), jax.random.fold_in(seeds[6], 1), 0, BATCH - 1).astype(jnp.int32)
    layout = draw_layout(jax.random.fold_in(seeds[8], 71), 0)
    return dict(queries=queries, keys=keys, values=values, grad_out=grad_out, layer_input=layer_input, basis_store=basis_store, owner=owner, layout=layout)


masked_score = -1.0e30


def sequence_grads(queries, keys, values, grad_out, layout):
    scale = HEAD_DIM ** -0.5
    runs = HEADS // HEAD_DEV
    query_blocks = queries.reshape(NQB, BLOCK, HEADS, HEAD_DIM)
    grad_blocks = grad_out.reshape(NQB, BLOCK, HEADS, HEAD_DIM)
    key_blocks = keys.reshape(NQB, BLOCK, KV_HEADS, HEAD_DIM)
    value_blocks = values.reshape(NQB, BLOCK, KV_HEADS, HEAD_DIM)
    kv_of_head = (jnp.arange(HEADS, dtype=jnp.int32) // GROUP)[:, None]
    run_of_head = (jnp.arange(HEADS, dtype=jnp.int32) // HEAD_DEV)[:, None]
    rows = lax.broadcasted_iota(jnp.int32, (BLOCK, BLOCK), 0)
    columns = lax.broadcasted_iota(jnp.int32, (BLOCK, BLOCK), 1)
    pattern = columns <= rows

    def step(carry, inputs):
        key_part, value_part = carry
        query_block, query_rows, grad_rows = inputs
        listed = lax.dynamic_index_in_dim(layout, query_block, 1, keepdims=False)
        valid = listed >= 0
        safe = jnp.maximum(listed, 0).astype(jnp.int32)
        key_sel = key_blocks[safe, :, kv_of_head, :].astype(jnp.float32)
        value_sel = value_blocks[safe, :, kv_of_head, :].astype(jnp.float32)
        query_f = query_rows.astype(jnp.float32)
        grad_f = grad_rows.astype(jnp.float32)
        scores = jnp.einsum("qhd,hskd->hqsk", query_f, key_sel) * scale
        earlier = (safe < query_block)[:, None, :, None]
        same = (safe == query_block)[:, None, :, None]
        visible = valid[:, None, :, None] & (earlier | (same & pattern[None, :, None, :]))
        scores = jnp.where(visible, scores, masked_score)
        top = jnp.max(scores, axis=(2, 3), keepdims=True)
        raw = jnp.exp(scores - top)
        weights = raw / jnp.sum(raw, axis=(2, 3), keepdims=True)
        weights_low = weights.astype(jnp.bfloat16).astype(jnp.float32)
        attended = jnp.einsum("hqsk,hskd->qhd", weights_low, value_sel)
        delta = jnp.sum(grad_f * attended, axis=2)
        dweights = jnp.einsum("qhd,hskd->hqsk", grad_f, value_sel)
        dscores = weights * (dweights - jnp.transpose(delta)[:, :, None, None])
        dscores_low = dscores.astype(jnp.bfloat16).astype(jnp.float32)
        query_grad = (jnp.einsum("hqsk,hskd->qhd", dscores_low, key_sel) * scale).astype(jnp.bfloat16)
        key_terms = jnp.einsum("hqsk,qhd->hskd", dscores_low, query_f) * scale
        value_terms = jnp.einsum("hqsk,qhd->hskd", weights_low, grad_f)
        key_part = key_part.at[run_of_head, safe].add(key_terms)
        value_part = value_part.at[run_of_head, safe].add(value_terms)
        return (key_part, value_part), query_grad

    zeros_part = jnp.zeros((runs, NQB, BLOCK, HEAD_DIM), jnp.float32)
    (key_part, value_part), query_grad = lax.scan(step, (zeros_part, zeros_part), (jnp.arange(NQB, dtype=jnp.int32), query_blocks, grad_blocks))
    query_grad = query_grad.reshape(SEQ_LEN, HEADS * HEAD_DIM)

    def fold_runs(part):
        rounded = lax.optimization_barrier(part.astype(jnp.bfloat16)).astype(jnp.float32)
        summed = jnp.sum(rounded.reshape(KV_HEADS, runs // KV_HEADS, SEQ_LEN, HEAD_DIM), axis=1)
        return jnp.transpose(summed, (1, 0, 2)).reshape(SEQ_LEN, KV_HEADS * HEAD_DIM)

    kv_grad = jnp.concatenate([fold_runs(key_part), fold_runs(value_part)], axis=1).astype(jnp.bfloat16)
    return query_grad, kv_grad


def reference(queries, keys, values, grad_out, layer_input, basis_store, owner, layout):
    pieces = []
    for index in range(2 * KV_HEADS):
        chosen = lax.dynamic_index_in_dim(basis_store, owner[index].astype(jnp.int32), 0, keepdims=False)
        pieces.append(chosen[index * HEAD_DIM:(index + 1) * HEAD_DIM])
    basis = jnp.concatenate(pieces, axis=0)

    def one_sequence(total, inputs):
        query_seq, key_seq, value_seq, grad_seq, input_seq = inputs
        query_grad, kv_grad = sequence_grads(query_seq, key_seq, value_seq, grad_seq, layout)
        projected = jnp.dot(kv_grad, basis, preferred_element_type=jnp.float32).astype(jnp.bfloat16)
        total = total + jnp.dot(input_seq.T, projected, preferred_element_type=jnp.float32)
        return total, query_grad

    start = jnp.zeros((FEATURES, RANK), jnp.float32)
    total, grad_query = lax.scan(one_sequence, start, (queries, keys, values, grad_out, layer_input))
    return grad_query, total / BATCH
```

```python
import math
from functools import partial

import jax
import jax.numpy as jnp
from jax import lax
from jax.experimental import pallas as pl
from jax.experimental.pallas import tpu as pltpu
from jax.sharding import PartitionSpec as P

HEADS = 32
KV_HEADS = 4
HEAD_DIM = 128
BLOCK = 128
GROUP = HEADS // KV_HEADS
UNROLL = 2
MASKED = -1e30

bf16 = jnp.bfloat16
f32 = jnp.float32
NT = (((1,), (1,)), ((), ()))
NN = (((1,), (0,)), ((), ()))
TN = (((0,), (0,)), ((), ()))


def mm(a, b, dims=NN):
    return lax.dot_general(a, b, dims, preferred_element_type=f32)


def attention_kernel(
    layout_ref, owner_ref, q_ref, do_ref, *refs, chips, dp_count, blocks, slots
):
    count = 2 * chips
    k_refs, refs = refs[:count], refs[count:]
    v_refs, refs = refs[:count], refs[count:]
    bk_refs, refs = refs[:dp_count], refs[dp_count:]
    bv_refs, refs = refs[:dp_count], refs[dp_count:]
    dq_ref, keep_ref, send_ref, kbuf, ktbuf, vbuf, dk_acc, dv_acc, basis, send_acc = refs

    kv_head = pl.program_id(0)
    place = lax.axis_index("seq")
    chip = place // 2
    core = lax.rem(place, 2)
    me = lax.axis_index("dp")
    scale = HEAD_DIM ** (-0.5)
    to_exp2 = scale * math.log2(math.e)

    for index in range(count):
        block = k_refs[index][...]
        kbuf[index] = block
        ktbuf[index] = block.T
        vbuf[index] = v_refs[index][...]
    dk_acc[...] = jnp.zeros_like(dk_acc)
    dv_acc[...] = jnp.zeros_like(dv_acc)

    own_k = lax.rem(me - owner_ref[kv_head] + dp_count, dp_count)
    own_v = lax.rem(me - owner_ref[KV_HEADS + kv_head] + dp_count, dp_count)
    for index in range(dp_count):

        @pl.when(own_k == index)
        def _():
            basis[:HEAD_DIM] = bk_refs[index][...]

        @pl.when(own_v == index)
        def _():
            basis[HEAD_DIM:] = bv_refs[index][...]

    rows = lax.broadcasted_iota(jnp.int32, (BLOCK, BLOCK), 0)
    columns = lax.broadcasted_iota(jnp.int32, (BLOCK, BLOCK), 1)
    causal = rows <= columns

    def heads_step(step, carry):
        lists = []
        for unit in range(UNROLL):
            head = kv_head * GROUP + step * UNROLL + unit
            base = (head * blocks + place) * slots
            listed = [layout_ref[base + slot] for slot in range(slots)]
            length = sum([(entry >= 0).astype(jnp.int32) for entry in listed])
            lists.append((listed, length))
        most = lists[0][1]
        for _, length in lists[1:]:
            most = jnp.maximum(most, length)

        def work(width):
            for unit in range(UNROLL):
                listed, length = lists[unit]
                lane = pl.ds(pl.multiple_of((step * UNROLL + unit) * HEAD_DIM, HEAD_DIM), HEAD_DIM)
                q = q_ref[:, lane]
                do = do_ref[:, lane]
                spots = [0]
                valid = [None]
                for slot in range(1, width):
                    entry = listed[slot - 1]
                    ok = slot < length
                    spot = (chip - entry // 2) + chips * (lax.rem(entry + core, 2))
                    spots.append(jnp.where(ok, spot, 0))
                    valid.append(ok)
                ks = jnp.concatenate([kbuf[spot] for spot in spots], axis=0)
                vs = jnp.concatenate([vbuf[spot] for spot in spots], axis=0)
                scores = mm(ks, q, NT) * to_exp2
                pieces = []
                for slot in range(width):
                    piece = scores[slot * BLOCK : (slot + 1) * BLOCK]
                    if slot == 0:
                        piece = jnp.where(causal, piece, MASKED)
                    else:
                        piece = jnp.where(valid[slot], piece, MASKED)
                    pieces.append(piece)
                scores = jnp.concatenate(pieces, axis=0)
                top = jnp.max(scores, axis=0, keepdims=True)
                raw = jnp.exp2(scores - top)
                weights = raw * (1.0 / jnp.sum(raw, axis=0, keepdims=True))
                low = weights.astype(bf16)
                dweights = mm(vs, do, NT)
                delta = jnp.sum(low.astype(f32) * dweights, axis=0, keepdims=True)
                dscores = (weights * (dweights - delta)).astype(bf16)
                dk = mm(dscores, q)
                dv = mm(low, do)
                kt = jnp.concatenate([ktbuf[spot] for spot in spots], axis=1)
                dq = (mm(kt, dscores) * scale).astype(bf16)
                dq_ref[:, lane] = dq.T
                for slot in range(width):
                    part = slice(slot * BLOCK, (slot + 1) * BLOCK)
                    dk_acc[spots[slot]] += dk[part]
                    dv_acc[spots[slot]] += dv[part]

        for width in range(1, slots + 1):
            pl.when(most == width)(partial(work, width))
        return carry

    lax.fori_loop(0, GROUP // UNROLL, heads_step, 0)

    chosen = basis[...]
    for index in range(count):
        grads = jnp.concatenate(
            [(dk_acc[index] * scale).astype(bf16), dv_acc[index].astype(bf16)], axis=1
        )
        term = mm(grads, chosen)
        target = keep_ref if index < chips else send_acc
        spot = slice((index % chips) * BLOCK, (index % chips + 1) * BLOCK)

        @pl.when(kv_head == 0)
        def _():
            target[spot] = term

        @pl.when(kv_head > 0)
        def _():
            target[spot] += term

    @pl.when(kv_head == KV_HEADS - 1)
    def _():
        send_ref[...] = send_acc[...].astype(bf16)


def attention(layout, owner, queries, grads, kv_parts, bases, blocks, slots):
    count = len(kv_parts)
    chips = count // 2
    rank = bases[0].shape[1]
    width = GROUP * HEAD_DIM
    body = partial(
        attention_kernel, chips=chips, dp_count=len(bases), blocks=blocks, slots=slots
    )
    wide = pl.BlockSpec((BLOCK, width), lambda g, *_: (0, g))
    key_spec = pl.BlockSpec((BLOCK, HEAD_DIM), lambda g, *_: (0, g))
    value_spec = pl.BlockSpec((BLOCK, HEAD_DIM), lambda g, *_: (0, KV_HEADS + g))
    basis_k = pl.BlockSpec((HEAD_DIM, rank), lambda g, *_: (g, 0))
    basis_v = pl.BlockSpec((HEAD_DIM, rank), lambda g, *_: (KV_HEADS + g, 0))
    whole = pl.BlockSpec((chips * BLOCK, rank), lambda g, *_: (0, 0))
    pairs = HEADS * 3
    return pl.pallas_call(
        body,
        grid_spec=pltpu.PrefetchScalarGridSpec(
            num_scalar_prefetch=2,
            grid=(KV_HEADS,),
            in_specs=[wide, wide]
            + [key_spec] * count
            + [value_spec] * count
            + [basis_k] * len(bases)
            + [basis_v] * len(bases),
            out_specs=[wide, whole, whole],
            scratch_shapes=[
                pltpu.VMEM((count, BLOCK, HEAD_DIM), bf16),
                pltpu.VMEM((count, HEAD_DIM, BLOCK), bf16),
                pltpu.VMEM((count, BLOCK, HEAD_DIM), bf16),
                pltpu.VMEM((count, BLOCK, HEAD_DIM), f32),
                pltpu.VMEM((count, BLOCK, HEAD_DIM), f32),
                pltpu.VMEM((2 * HEAD_DIM, rank), bf16),
                pltpu.VMEM((chips * BLOCK, rank), f32),
            ],
        ),
        out_shape=[
            jax.ShapeDtypeStruct((BLOCK, HEADS * HEAD_DIM), bf16),
            jax.ShapeDtypeStruct((chips * BLOCK, rank), f32),
            jax.ShapeDtypeStruct((chips * BLOCK, rank), bf16),
        ],
        compiler_params=pltpu.CompilerParams(vmem_limit_bytes=56 * 1024 * 1024),
        cost_estimate=pl.CostEstimate(
            flops=pairs * 10 * BLOCK**3, bytes_accessed=8 << 20, transcendentals=pairs * BLOCK**2
        ),
        name="attention_backward",
    )(
        layout,
        owner,
        queries,
        grads,
        *kv_parts,
        *kv_parts,
        *bases,
        *bases,
    )


def fold_kernel(keep_ref, came_ref, own_ref, *send_refs):
    own_ref[...] = keep_ref[:BLOCK] + came_ref[:BLOCK].astype(f32)
    for index, send_ref in enumerate(send_refs):
        rows = slice((index + 1) * BLOCK, (index + 2) * BLOCK)
        send_ref[...] = (keep_ref[rows] + came_ref[rows].astype(f32)).astype(bf16)


def fold(keep, came, chips):
    rank = keep.shape[1]
    return pl.pallas_call(
        fold_kernel,
        out_shape=[jax.ShapeDtypeStruct((BLOCK, rank), f32)]
        + [jax.ShapeDtypeStruct((BLOCK, rank), bf16)] * (chips - 1),
        compiler_params=pltpu.CompilerParams(vmem_limit_bytes=32 * 1024 * 1024),
        name="fold_parts",
    )(keep, came)


def outer_kernel(*refs, chips):
    x_refs, refs = refs[:chips], refs[chips:]
    p_refs, refs = refs[:chips], refs[chips:]
    keep_ref, send_ref = refs
    core = lax.rem(lax.axis_index("seq"), 2)
    half = keep_ref.shape[0]

    def product(which):
        columns = pl.ds(pl.multiple_of(which * half, half), half)
        inputs = jnp.concatenate([ref[:, columns] for ref in x_refs], axis=0)
        projected = jnp.concatenate([ref[...] for ref in p_refs], axis=0)
        return mm(inputs, projected, TN)

    send_ref[...] = product(1 - core).astype(bf16)
    keep_ref[...] = product(core)


def outer(x_parts, p_parts):
    chips = len(x_parts)
    features = x_parts[0].shape[1]
    rank = p_parts[0].shape[1]
    return pl.pallas_call(
        partial(outer_kernel, chips=chips),
        out_shape=[
            jax.ShapeDtypeStruct((features // 2, rank), f32),
            jax.ShapeDtypeStruct((features // 2, rank), bf16),
        ],
        compiler_params=pltpu.CompilerParams(vmem_limit_bytes=32 * 1024 * 1024),
        name="outer_product",
    )(*x_parts, *p_parts)


def local(queries, keys, values, grad_out, layer_input, basis_store, owner, layout):
    seq_count = lax.axis_size("seq")
    dp_count = lax.axis_size("dp")
    chips = seq_count // 2
    place = lax.axis_index("seq")
    chip = place // 2
    blocks, slots = layout.shape[1], layout.shape[2]

    def pair(x):
        return lax.ppermute(x, "seq", [(i, i ^ 1) for i in range(seq_count)])

    def up(x, step):
        moves = [(i, i + 2 * step) for i in range(seq_count) if i + 2 * step < seq_count]
        return lax.ppermute(x, "seq", moves)

    def down(x, step):
        moves = [(i, i - 2 * step) for i in range(seq_count) if i >= 2 * step]
        return lax.ppermute(x, "seq", moves)

    def around(x, step):
        moves = [(i, (i + 2 * step) % seq_count) for i in range(seq_count)]
        return lax.ppermute(x, "seq", moves)

    def across(x, step):
        return lax.ppermute(x, "dp", [(i, (i + step) % dp_count) for i in range(dp_count)])

    kv = jnp.concatenate([keys[0], values[0]], axis=1)
    same = [kv] + [up(kv, step) for step in range(1, chips)]
    other = [pair(part) for part in same]

    basis = basis_store[0]
    bases = [basis] + [across(basis, step) for step in range(1, dp_count)]

    features = layer_input.shape[2] // chips

    def columns(step):
        target = lax.rem(chip + step, chips)
        return lax.dynamic_slice_in_dim(layer_input[0], target * features, features, 1)

    x_parts = [columns(0)] + [around(columns(step), step) for step in range(1, chips)]

    grad_query, keep, send = attention(
        layout.reshape(-1),
        owner,
        queries[0],
        grad_out[0],
        same + other,
        bases,
        blocks,
        slots,
    )

    own, *sends = fold(keep, pair(send), chips)
    total = own
    for step in range(1, chips):
        total = total + down(sends[step - 1], step).astype(f32)
    projected = total.astype(bf16)
    p_parts = [projected] + [around(projected, step) for step in range(1, chips)]
    kept, sent = outer(x_parts, p_parts)
    partial_rank = kept + pair(sent).astype(f32)
    low = partial_rank.astype(bf16)
    for step in range(1, dp_count):
        partial_rank = partial_rank + across(low, step).astype(f32)
    lowrank_grad = partial_rank / dp_count
    return (grad_query[None], lowrank_grad)


def solution(mesh):
    in_specs = (
        P("dp", "seq", None),
        P("dp", "seq", None),
        P("dp", "seq", None),
        P("dp", "seq", None),
        P("dp", "seq", None),
        P("dp", None, None),
        P(),
        P(),
    )
    out_specs = (P("dp", "seq", None), P("seq", None))
    return jax.shard_map(local, mesh=mesh, in_specs=in_specs, out_specs=out_specs, check_vma=False)
```

```python
import math
from functools import partial

import jax
import jax.numpy as jnp
from jax import lax
from jax.experimental import pallas as pl
from jax.experimental.pallas import tpu as pltpu
from jax.sharding import PartitionSpec as P

HEADS = 32
KV_HEADS = 4
HEAD_DIM = 128
BLOCK = 128
GROUP = HEADS // KV_HEADS
UNROLL = 4
CHUNKS = 1
VMEM_ATT = 24 * 1024 * 1024
MASKED = -1e30

bf16 = jnp.bfloat16
f32 = jnp.float32
NT = (((1,), (1,)), ((), ()))
NN = (((1,), (0,)), ((), ()))
TN = (((0,), (0,)), ((), ()))


def mm(a, b, dims=NN):
    return lax.dot_general(a, b, dims, preferred_element_type=f32)


def lists_by_length(layout, place, chips):
    slots = layout.shape[2]
    chip, core = place // 2, lax.rem(place, 2)
    lists = lax.dynamic_slice_in_dim(layout, place, 1, 1)[:, 0]
    length = jnp.sum((lists >= 0).astype(jnp.int32), axis=1)
    spots = (chip - lists // 2) + chips * ((lists + core) % 2)
    earlier = jnp.arange(slots, dtype=jnp.int32)[None] < length[:, None] - 1
    spots = jnp.where(earlier, spots, 0)
    within = jnp.arange(HEADS, dtype=jnp.int32) % GROUP
    table = jnp.concatenate([within[:, None], length[:, None], spots[:, : slots - 1]], axis=1)
    table = table.reshape(KV_HEADS, GROUP, slots + 1)
    size = length.reshape(KV_HEADS, GROUP)
    inside = jnp.arange(GROUP, dtype=jnp.int32)
    mine, others = size[:, :, None], size[:, None, :]
    ahead = (others > mine) | ((others == mine) & (inside[None, None, :] < inside[None, :, None]))
    rank = jnp.sum(ahead.astype(jnp.int32), axis=2)
    chosen = rank[:, :, None] == inside[None, None, :]
    ordered = jnp.sum(jnp.where(chosen[..., None], table[:, :, None, :], 0), axis=1)
    return ordered.reshape(-1)


def attention_kernel(table_ref, q_ref, do_ref, *refs, chips, slots, first, heads):
    count = 2 * chips
    kv_refs, refs = refs[:count], refs[count:]
    dq_ref, grads_ref, kbuf, ktbuf, vbuf, dk_acc, dv_acc = refs
    row = slots + 1
    scale = HEAD_DIM ** (-0.5)
    to_exp2 = scale * math.log2(math.e)
    rows = lax.broadcasted_iota(jnp.int32, (BLOCK, BLOCK), 0)
    columns = lax.broadcasted_iota(jnp.int32, (BLOCK, BLOCK), 1)
    causal = rows <= columns

    def one_kv_head(kv_head):
        k_lane = slice(kv_head * HEAD_DIM, (kv_head + 1) * HEAD_DIM)
        v_lane = slice((heads + kv_head) * HEAD_DIM, (heads + kv_head + 1) * HEAD_DIM)
        for index in range(count):
            block = kv_refs[index][:, k_lane]
            kbuf[index] = block
            ktbuf[index] = block.T
            vbuf[index] = kv_refs[index][:, v_lane]
        dk_acc[...] = jnp.zeros_like(dk_acc)
        dv_acc[...] = jnp.zeros_like(dv_acc)

        def heads_step(step, carry):
            base = ((first + kv_head) * GROUP + step * UNROLL) * row
            most = table_ref[base + 1]

            def work(width):
                units = range(UNROLL)
                lanes_in, lanes_out, spots, valid = [], [], [], []
                for unit in units:
                    start = base + unit * row
                    head = table_ref[start]
                    length = table_ref[start + 1]
                    spots.append([0] + [table_ref[start + 1 + slot] for slot in range(1, width)])
                    valid.append([None] + [slot < length for slot in range(1, width)])
                    at_in = ((first + kv_head) * GROUP + head) * HEAD_DIM
                    at_out = (kv_head * GROUP + head) * HEAD_DIM
                    lanes_in.append(pl.ds(pl.multiple_of(at_in, HEAD_DIM), HEAD_DIM))
                    lanes_out.append(pl.ds(pl.multiple_of(at_out, HEAD_DIM), HEAD_DIM))
                qs = [q_ref[:, lanes_in[unit]] for unit in units]
                dos = [do_ref[:, lanes_in[unit]] for unit in units]
                scores, dweights = [], []
                for unit in units:
                    ks = jnp.concatenate([kbuf[spot] for spot in spots[unit]], axis=0)
                    scores.append(mm(ks, qs[unit], NT))
                for unit in units:
                    vs = jnp.concatenate([vbuf[spot] for spot in spots[unit]], axis=0)
                    dweights.append(mm(vs, dos[unit], NT))
                lows, dlows = [], []
                for unit in units:
                    pieces = []
                    for slot in range(width):
                        piece = scores[unit][slot * BLOCK : (slot + 1) * BLOCK] * to_exp2
                        shown = causal if slot == 0 else valid[unit][slot]
                        pieces.append(jnp.where(shown, piece, MASKED))
                    masked = jnp.concatenate(pieces, axis=0)
                    top = jnp.max(masked, axis=0, keepdims=True)
                    raw = jnp.exp2(masked - top)
                    weights = raw * (1.0 / jnp.sum(raw, axis=0, keepdims=True))
                    delta = jnp.sum(weights * dweights[unit], axis=0, keepdims=True)
                    lows.append(weights.astype(bf16))
                    dlows.append((weights * (dweights[unit] - delta)).astype(bf16))
                for unit in units:
                    kt = jnp.concatenate([ktbuf[spot] for spot in spots[unit]], axis=1)
                    dq_ref[:, lanes_out[unit]] = (mm(kt, dlows[unit]) * scale).astype(bf16).T
                dk_acc[0] += mm(
                    jnp.concatenate([dlow[:BLOCK] for dlow in dlows], axis=1),
                    jnp.concatenate(qs, axis=0),
                )
                dv_acc[0] += mm(
                    jnp.concatenate([low[:BLOCK] for low in lows], axis=1),
                    jnp.concatenate(dos, axis=0),
                )
                if width > 1:
                    for unit in units:
                        dk = mm(dlows[unit][BLOCK:], qs[unit])
                        dv = mm(lows[unit][BLOCK:], dos[unit])
                        for slot in range(1, width):
                            part = slice((slot - 1) * BLOCK, slot * BLOCK)
                            dk_acc[spots[unit][slot]] += dk[part]
                            dv_acc[spots[unit][slot]] += dv[part]

            for width in range(1, slots + 1):
                pl.when(most == width)(partial(work, width))
            return carry

        lax.fori_loop(0, GROUP // UNROLL, heads_step, 0)
        for index in range(count):
            at = slice(index * BLOCK, (index + 1) * BLOCK)
            grads_ref[at, k_lane] = (dk_acc[index] * scale).astype(bf16)
            grads_ref[at, v_lane] = dv_acc[index].astype(bf16)

    for kv_head in range(heads):
        one_kv_head(kv_head)


def attention(table, queries, grads, kv_parts, slots, first, heads):
    count = len(kv_parts)
    body = partial(attention_kernel, chips=count // 2, slots=slots, first=first, heads=heads)
    whole = pl.BlockSpec(memory_space=pltpu.VMEM)
    pairs = heads * GROUP * 3
    return pl.pallas_call(
        body,
        in_specs=[pl.BlockSpec(memory_space=pltpu.SMEM)] + [whole] * (2 + count),
        out_specs=[whole, whole],
        out_shape=[
            jax.ShapeDtypeStruct((BLOCK, heads * GROUP * HEAD_DIM), bf16),
            jax.ShapeDtypeStruct((count * BLOCK, 2 * heads * HEAD_DIM), bf16),
        ],
        scratch_shapes=[
            pltpu.VMEM((count, BLOCK, HEAD_DIM), bf16),
            pltpu.VMEM((count, HEAD_DIM, BLOCK), bf16),
            pltpu.VMEM((count, BLOCK, HEAD_DIM), bf16),
            pltpu.VMEM((count, BLOCK, HEAD_DIM), f32),
            pltpu.VMEM((count, BLOCK, HEAD_DIM), f32),
        ],
        compiler_params=pltpu.CompilerParams(vmem_limit_bytes=VMEM_ATT),
        cost_estimate=pl.CostEstimate(
            flops=pairs * 100 * BLOCK**3, bytes_accessed=4 << 20, transcendentals=pairs * BLOCK**2
        ),
        name="attention_backward",
    )(table, queries, grads, *kv_parts)

def project_kernel(mine_ref, other_ref, *refs, chips, chunks):
    grads_refs, refs = refs[:chunks], refs[chunks:]
    keep_ref, send_ref, basis = refs
    half = mine_ref.shape[0]
    core = lax.rem(lax.axis_index("seq"), 2)

    @pl.when(core == 0)
    def _():
        basis[:half] = mine_ref[...]
        basis[half:] = other_ref[...]

    @pl.when(core == 1)
    def _():
        basis[:half] = other_ref[...]
        basis[half:] = mine_ref[...]

    chosen = basis[...]
    part = grads_refs[0].shape[1] // 2
    tall = min(chips, 4) * BLOCK

    def product(start):
        rows = slice(start, start + tall)
        keys = [ref[rows, :part] for ref in grads_refs]
        values = [ref[rows, part:] for ref in grads_refs]
        return mm(jnp.concatenate(keys + values, axis=1), chosen)

    for start in range(0, chips * BLOCK, tall):
        send_ref[start : start + tall] = product(chips * BLOCK + start).astype(bf16)
        keep_ref[start : start + tall] = product(start)


def project(mine, other, grads, chips):
    rank = mine.shape[1]
    return pl.pallas_call(
        partial(project_kernel, chips=chips, chunks=len(grads)),
        out_shape=[
            jax.ShapeDtypeStruct((chips * BLOCK, rank), f32),
            jax.ShapeDtypeStruct((chips * BLOCK, rank), bf16),
        ],
        scratch_shapes=[pltpu.VMEM((2 * mine.shape[0], rank), bf16)],
        compiler_params=pltpu.CompilerParams(vmem_limit_bytes=32 * 1024 * 1024),
        name="project",
    )(mine, other, *grads)


def fold_kernel(keep_ref, came_ref, own_ref, *send_refs):
    own_ref[...] = keep_ref[:BLOCK] + came_ref[:BLOCK].astype(f32)
    for index, send_ref in enumerate(send_refs):
        rows = slice((index + 1) * BLOCK, (index + 2) * BLOCK)
        send_ref[...] = (keep_ref[rows] + came_ref[rows].astype(f32)).astype(bf16)


def fold(keep, came, chips):
    rank = keep.shape[1]
    return pl.pallas_call(
        fold_kernel,
        out_shape=[jax.ShapeDtypeStruct((BLOCK, rank), f32)]
        + [jax.ShapeDtypeStruct((BLOCK, rank), bf16)] * (chips - 1),
        compiler_params=pltpu.CompilerParams(vmem_limit_bytes=32 * 1024 * 1024),
        name="fold_parts",
    )(keep, came)


def outer_kernel(*refs, chips):
    x_refs, refs = refs[:chips], refs[chips:]
    p_refs, refs = refs[:chips], refs[chips:]
    keep_ref, send_ref = refs
    core = lax.rem(lax.axis_index("seq"), 2)
    half = keep_ref.shape[0]

    def product(which):
        columns = pl.ds(pl.multiple_of(which * half, half), half)
        inputs = jnp.concatenate([ref[:, columns] for ref in x_refs], axis=0)
        projected = jnp.concatenate([ref[...] for ref in p_refs], axis=0)
        return mm(inputs, projected, TN)

    send_ref[...] = product(1 - core).astype(bf16)
    keep_ref[...] = product(core)


def outer(x_parts, p_parts):
    chips = len(x_parts)
    features = x_parts[0].shape[1]
    rank = p_parts[0].shape[1]
    return pl.pallas_call(
        partial(outer_kernel, chips=chips),
        out_shape=[
            jax.ShapeDtypeStruct((features // 2, rank), f32),
            jax.ShapeDtypeStruct((features // 2, rank), bf16),
        ],
        compiler_params=pltpu.CompilerParams(vmem_limit_bytes=32 * 1024 * 1024),
        name="outer_product",
    )(*x_parts, *p_parts)


def local(queries, keys, values, grad_out, layer_input, basis_store, owner, layout):
    seq_count = lax.axis_size("seq")
    dp_count = lax.axis_size("dp")
    chips = seq_count // 2
    place = lax.axis_index("seq")
    chip, core = place // 2, lax.rem(place, 2)
    me = lax.axis_index("dp")
    slots = layout.shape[2]
    rank = basis_store.shape[2]

    def pair(x):
        return lax.ppermute(x, "seq", [(i, i ^ 1) for i in range(seq_count)])

    def up(x, step):
        moves = [(i, i + 2 * step) for i in range(seq_count) if i + 2 * step < seq_count]
        return lax.ppermute(x, "seq", moves)

    def down(x, step):
        moves = [(i, i - 2 * step) for i in range(seq_count) if i >= 2 * step]
        return lax.ppermute(x, "seq", moves)

    def around(x, step):
        moves = [(i, (i + 2 * step) % seq_count) for i in range(seq_count)]
        return lax.ppermute(x, "seq", moves)

    def across(x, step):
        return lax.ppermute(x, "dp", [(i, i ^ step) for i in range(dp_count)])

    heads = KV_HEADS // CHUNKS
    part = heads * HEAD_DIM

    def gathered(chunk):
        columns = slice(chunk * part, (chunk + 1) * part)
        kv = jnp.concatenate([keys[0][:, columns], values[0][:, columns]], axis=1)
        same = [kv] + [up(kv, step) for step in range(1, chips)]
        return same + [pair(piece) for piece in same]

    kv_parts = [gathered(chunk) for chunk in range(CHUNKS)]
    table = lists_by_length(layout, place, chips)

    pieces = KV_HEADS
    half = lax.dynamic_slice_in_dim(basis_store[0], core * pieces * HEAD_DIM, pieces * HEAD_DIM, 0)
    owners = lax.dynamic_slice_in_dim(owner, core * pieces, pieces, 0)
    from_where = (owners ^ me)[:, None, None]
    mine = half.reshape(pieces, HEAD_DIM, rank)
    for step in range(1, dp_count):
        came = across(half, step).reshape(pieces, HEAD_DIM, rank)
        mine = jnp.where(from_where == step, came, mine)
    mine = mine.reshape(pieces * HEAD_DIM, rank)
    other = pair(mine)

    features = layer_input.shape[2] // chips

    def columns(step):
        target = lax.rem(chip + step, chips)
        return lax.dynamic_slice_in_dim(layer_input[0], target * features, features, 1)

    x_parts = [columns(0)] + [around(columns(step), step) for step in range(1, chips)]

    query_grads, grads = [], []
    for chunk in range(CHUNKS):
        query_grad, grad = attention(
            table, queries[0], grad_out[0], kv_parts[chunk], slots, chunk * heads, heads
        )
        query_grads.append(query_grad)
        grads.append(grad)
    grad_query = jnp.concatenate(query_grads, axis=1)

    keep, send = project(mine, other, grads, chips)
    (send, x_parts) = lax.optimization_barrier((send, x_parts))
    own, *sends = fold(keep, pair(send), chips)
    total = own
    for step in range(1, chips):
        total = total + down(sends[step - 1], step).astype(f32)
    projected = total.astype(bf16)
    p_parts = [projected] + [around(projected, step) for step in range(1, chips)]
    kept, sent = outer(x_parts, p_parts)
    partial_rank = kept + pair(sent).astype(f32)
    low = partial_rank.astype(bf16)
    for step in range(1, dp_count):
        partial_rank = partial_rank + across(low, step).astype(f32)
    lowrank_grad = partial_rank / dp_count
    return (grad_query[None], lowrank_grad)


def solution(mesh):
    in_specs = (
        P("dp", "seq", None),
        P("dp", "seq", None),
        P("dp", "seq", None),
        P("dp", "seq", None),
        P("dp", "seq", None),
        P("dp", None, None),
        P(),
        P(),
    )
    out_specs = (P("dp", "seq", None), P("seq", None))
    return jax.shard_map(local, mesh=mesh, in_specs=in_specs, out_specs=out_specs, check_vma=False)
```

```python
import math
from functools import partial

import jax
import jax.numpy as jnp
from jax import lax
from jax.experimental import pallas as pl
from jax.experimental.pallas import tpu as pltpu
from jax.sharding import PartitionSpec as P

HEADS = 32
KV_HEADS = 4
HEAD_DIM = 128
BLOCK = 128
GROUP = HEADS // KV_HEADS
UNROLL = 4
CHUNKS = 2
VMEM_ATT = 24 * 1024 * 1024
MASKED = -1e30

bf16 = jnp.bfloat16
f32 = jnp.float32
NT = (((1,), (1,)), ((), ()))
NN = (((1,), (0,)), ((), ()))
TN = (((0,), (0,)), ((), ()))


def mm(a, b, dims=NN):
    return lax.dot_general(a, b, dims, preferred_element_type=f32)


def lists_by_length(layout, place, chips):
    slots = layout.shape[2]
    chip, core = place // 2, lax.rem(place, 2)
    lists = lax.dynamic_slice_in_dim(layout, place, 1, 1)[:, 0]
    length = jnp.sum((lists >= 0).astype(jnp.int32), axis=1)
    spots = (chip - lists // 2) + chips * ((lists + core) % 2)
    earlier = jnp.arange(slots, dtype=jnp.int32)[None] < length[:, None] - 1
    spots = jnp.where(earlier, spots, 0)
    within = jnp.arange(HEADS, dtype=jnp.int32) % GROUP
    table = jnp.concatenate([within[:, None], length[:, None], spots[:, : slots - 1]], axis=1)
    table = table.reshape(KV_HEADS, GROUP, slots + 1)
    size = length.reshape(KV_HEADS, GROUP)
    inside = jnp.arange(GROUP, dtype=jnp.int32)
    mine, others = size[:, :, None], size[:, None, :]
    ahead = (others > mine) | ((others == mine) & (inside[None, None, :] < inside[None, :, None]))
    rank = jnp.sum(ahead.astype(jnp.int32), axis=2)
    chosen = rank[:, :, None] == inside[None, None, :]
    ordered = jnp.sum(jnp.where(chosen[..., None], table[:, :, None, :], 0), axis=1)
    return ordered.reshape(-1)


def attention_kernel(table_ref, q_ref, do_ref, *refs, chips, slots, first, heads):
    count = 2 * chips
    kv_refs, refs = refs[:count], refs[count:]
    dq_ref, grads_ref, kbuf, ktbuf, vbuf, dk_acc, dv_acc = refs
    row = slots + 1
    scale = HEAD_DIM ** (-0.5)
    to_exp2 = scale * math.log2(math.e)
    rows = lax.broadcasted_iota(jnp.int32, (BLOCK, BLOCK), 0)
    columns = lax.broadcasted_iota(jnp.int32, (BLOCK, BLOCK), 1)
    causal = rows <= columns

    def one_kv_head(kv_head):
        k_lane = slice(kv_head * HEAD_DIM, (kv_head + 1) * HEAD_DIM)
        v_lane = slice((heads + kv_head) * HEAD_DIM, (heads + kv_head + 1) * HEAD_DIM)
        for index in range(count):
            block = kv_refs[index][:, k_lane]
            kbuf[index] = block
            ktbuf[index] = block.T
            vbuf[index] = kv_refs[index][:, v_lane]
        dk_acc[...] = jnp.zeros_like(dk_acc)
        dv_acc[...] = jnp.zeros_like(dv_acc)

        def heads_step(step, carry):
            base = ((first + kv_head) * GROUP + step * UNROLL) * row
            most = table_ref[base + 1]

            def work(width):
                units = range(UNROLL)
                lanes_in, lanes_out, spots, valid = [], [], [], []
                for unit in units:
                    start = base + unit * row
                    head = table_ref[start]
                    length = table_ref[start + 1]
                    spots.append([0] + [table_ref[start + 1 + slot] for slot in range(1, width)])
                    valid.append([None] + [slot < length for slot in range(1, width)])
                    at_in = ((first + kv_head) * GROUP + head) * HEAD_DIM
                    at_out = (kv_head * GROUP + head) * HEAD_DIM
                    lanes_in.append(pl.ds(pl.multiple_of(at_in, HEAD_DIM), HEAD_DIM))
                    lanes_out.append(pl.ds(pl.multiple_of(at_out, HEAD_DIM), HEAD_DIM))
                qs = [q_ref[:, lanes_in[unit]] for unit in units]
                dos = [do_ref[:, lanes_in[unit]] for unit in units]
                scores, dweights = [], []
                for unit in units:
                    ks = jnp.concatenate([kbuf[spot] for spot in spots[unit]], axis=0)
                    scores.append(mm(ks, qs[unit], NT))
                for unit in units:
                    vs = jnp.concatenate([vbuf[spot] for spot in spots[unit]], axis=0)
                    dweights.append(mm(vs, dos[unit], NT))
                lows, dlows = [], []
                for unit in units:
                    pieces = []
                    for slot in range(width):
                        piece = scores[unit][slot * BLOCK : (slot + 1) * BLOCK] * to_exp2
                        shown = causal if slot == 0 else valid[unit][slot]
                        pieces.append(jnp.where(shown, piece, MASKED))
                    masked = jnp.concatenate(pieces, axis=0)
                    top = jnp.max(masked, axis=0, keepdims=True)
                    raw = jnp.exp2(masked - top)
                    weights = raw * (1.0 / jnp.sum(raw, axis=0, keepdims=True))
                    delta = jnp.sum(weights * dweights[unit], axis=0, keepdims=True)
                    lows.append(weights.astype(bf16))
                    dlows.append((weights * (dweights[unit] - delta)).astype(bf16))
                for unit in units:
                    kt = jnp.concatenate([ktbuf[spot] for spot in spots[unit]], axis=1)
                    dq_ref[:, lanes_out[unit]] = (mm(kt, dlows[unit]) * scale).astype(bf16).T
                dk_acc[0] += mm(
                    jnp.concatenate([dlow[:BLOCK] for dlow in dlows], axis=1),
                    jnp.concatenate(qs, axis=0),
                )
                dv_acc[0] += mm(
                    jnp.concatenate([low[:BLOCK] for low in lows], axis=1),
                    jnp.concatenate(dos, axis=0),
                )
                if width > 1:
                    for unit in units:
                        dk = mm(dlows[unit][BLOCK:], qs[unit])
                        dv = mm(lows[unit][BLOCK:], dos[unit])
                        for slot in range(1, width):
                            part = slice((slot - 1) * BLOCK, slot * BLOCK)
                            dk_acc[spots[unit][slot]] += dk[part]
                            dv_acc[spots[unit][slot]] += dv[part]

            for width in range(1, slots + 1):
                pl.when(most == width)(partial(work, width))
            return carry

        lax.fori_loop(0, GROUP // UNROLL, heads_step, 0)
        for index in range(count):
            at = slice(index * BLOCK, (index + 1) * BLOCK)
            grads_ref[at, k_lane] = (dk_acc[index] * scale).astype(bf16)
            grads_ref[at, v_lane] = dv_acc[index].astype(bf16)

    for kv_head in range(heads):
        one_kv_head(kv_head)


def attention(table, queries, grads, kv_parts, slots, first, heads):
    count = len(kv_parts)
    body = partial(attention_kernel, chips=count // 2, slots=slots, first=first, heads=heads)
    whole = pl.BlockSpec(memory_space=pltpu.VMEM)
    pairs = heads * GROUP * 3
    return pl.pallas_call(
        body,
        in_specs=[pl.BlockSpec(memory_space=pltpu.SMEM)] + [whole] * (2 + count),
        out_specs=[whole, whole],
        out_shape=[
            jax.ShapeDtypeStruct((BLOCK, heads * GROUP * HEAD_DIM), bf16),
            jax.ShapeDtypeStruct((count * BLOCK, 2 * heads * HEAD_DIM), bf16),
        ],
        scratch_shapes=[
            pltpu.VMEM((count, BLOCK, HEAD_DIM), bf16),
            pltpu.VMEM((count, HEAD_DIM, BLOCK), bf16),
            pltpu.VMEM((count, BLOCK, HEAD_DIM), bf16),
            pltpu.VMEM((count, BLOCK, HEAD_DIM), f32),
            pltpu.VMEM((count, BLOCK, HEAD_DIM), f32),
        ],
        compiler_params=pltpu.CompilerParams(vmem_limit_bytes=VMEM_ATT),
        cost_estimate=pl.CostEstimate(
            flops=pairs * 100 * BLOCK**3, bytes_accessed=4 << 20, transcendentals=pairs * BLOCK**2
        ),
        name="attention_backward",
    )(table, queries, grads, *kv_parts)

def project_kernel(mine_ref, other_ref, *refs, chips, chunks):
    grads_refs, refs = refs[:chunks], refs[chunks:]
    keep_ref, send_ref, basis = refs
    half = mine_ref.shape[0]
    core = lax.rem(lax.axis_index("seq"), 2)

    @pl.when(core == 0)
    def _():
        basis[:half] = mine_ref[...]
        basis[half:] = other_ref[...]

    @pl.when(core == 1)
    def _():
        basis[:half] = other_ref[...]
        basis[half:] = mine_ref[...]

    chosen = basis[...]
    part = grads_refs[0].shape[1] // 2
    tall = min(chips, 4) * BLOCK

    def product(start):
        rows = slice(start, start + tall)
        keys = [ref[rows, :part] for ref in grads_refs]
        values = [ref[rows, part:] for ref in grads_refs]
        return mm(jnp.concatenate(keys + values, axis=1), chosen)

    for start in range(0, chips * BLOCK, tall):
        send_ref[start : start + tall] = product(chips * BLOCK + start).astype(bf16)
        keep_ref[start : start + tall] = product(start)


def project(mine, other, grads, chips):
    rank = mine.shape[1]
    return pl.pallas_call(
        partial(project_kernel, chips=chips, chunks=len(grads)),
        out_shape=[
            jax.ShapeDtypeStruct((chips * BLOCK, rank), f32),
            jax.ShapeDtypeStruct((chips * BLOCK, rank), bf16),
        ],
        scratch_shapes=[pltpu.VMEM((2 * mine.shape[0], rank), bf16)],
        compiler_params=pltpu.CompilerParams(vmem_limit_bytes=32 * 1024 * 1024),
        name="project",
    )(mine, other, *grads)


def fold_kernel(keep_ref, came_ref, own_ref, *send_refs):
    own_ref[...] = keep_ref[:BLOCK] + came_ref[:BLOCK].astype(f32)
    for index, send_ref in enumerate(send_refs):
        rows = slice((index + 1) * BLOCK, (index + 2) * BLOCK)
        send_ref[...] = (keep_ref[rows] + came_ref[rows].astype(f32)).astype(bf16)


def fold(keep, came, chips):
    rank = keep.shape[1]
    return pl.pallas_call(
        fold_kernel,
        out_shape=[jax.ShapeDtypeStruct((BLOCK, rank), f32)]
        + [jax.ShapeDtypeStruct((BLOCK, rank), bf16)] * (chips - 1),
        compiler_params=pltpu.CompilerParams(vmem_limit_bytes=32 * 1024 * 1024),
        name="fold_parts",
    )(keep, came)


def outer_kernel(x_ref, *refs, dp_count):
    p_refs, refs = refs[:dp_count], refs[dp_count:]
    keep_ref, send_ref = refs
    core = lax.rem(lax.axis_index("seq"), 2)
    me = lax.axis_index("dp")
    half = keep_ref.shape[0]
    projected = jnp.concatenate([ref[...] for ref in p_refs], axis=0)

    def product(which):
        columns = pl.ds(pl.multiple_of(which * half, half), half)
        inputs = [x_ref[jnp.bitwise_xor(me, step), :, columns] for step in range(dp_count)]
        return mm(jnp.concatenate(inputs, axis=0), projected, TN)

    send_ref[...] = product(1 - core).astype(bf16)
    keep_ref[...] = product(core)


def outer(x_all, p_parts):
    features = x_all.shape[2]
    rank = p_parts[0].shape[1]
    return pl.pallas_call(
        partial(outer_kernel, dp_count=len(p_parts)),
        out_shape=[
            jax.ShapeDtypeStruct((features // 2, rank), f32),
            jax.ShapeDtypeStruct((features // 2, rank), bf16),
        ],
        compiler_params=pltpu.CompilerParams(vmem_limit_bytes=32 * 1024 * 1024),
        name="outer_product",
    )(x_all, *p_parts)


def deal_kernel(keep_ref, came_ref, own_ref, *refs):
    send_refs, total = refs[:-1], refs[-1]
    chips = len(send_refs) + 1
    chip = lax.axis_index("seq") // 2
    share = own_ref.shape[0]
    total[...] = keep_ref[...] + came_ref[...].astype(f32)

    def rows(step):
        return pl.ds(pl.multiple_of(lax.rem(chip + step, chips) * share, share), share)

    own_ref[...] = total[rows(0)]
    for step, send_ref in enumerate(send_refs, 1):
        send_ref[...] = total[rows(step)].astype(bf16)


def deal(keep, came, chips):
    share, rank = keep.shape[0] // chips, keep.shape[1]
    return pl.pallas_call(
        deal_kernel,
        out_shape=[jax.ShapeDtypeStruct((share, rank), f32)]
        + [jax.ShapeDtypeStruct((share, rank), bf16)] * (chips - 1),
        scratch_shapes=[pltpu.VMEM(keep.shape, f32)],
        compiler_params=pltpu.CompilerParams(vmem_limit_bytes=32 * 1024 * 1024),
        name="deal_rows",
    )(keep, came)


def lay_kernel(*refs):
    part_refs, out_ref = refs[:-1], refs[-1]
    me = lax.axis_index("dp")
    share = part_refs[0].shape[0]
    for step, part_ref in enumerate(part_refs):
        at = pl.multiple_of(jnp.bitwise_xor(me, step) * share, share)
        out_ref[pl.ds(at, share)] = part_ref[...].astype(f32) * (1.0 / len(part_refs))


def lay(parts):
    share, rank = parts[0].shape
    return pl.pallas_call(
        lay_kernel,
        out_shape=jax.ShapeDtypeStruct((share * len(parts), rank), f32),
        compiler_params=pltpu.CompilerParams(vmem_limit_bytes=32 * 1024 * 1024),
        name="lay_rows",
    )(*parts)


def local(queries, keys, values, grad_out, layer_input, basis_store, owner, layout):
    seq_count = lax.axis_size("seq")
    dp_count = lax.axis_size("dp")
    chips = seq_count // 2
    place = lax.axis_index("seq")
    chip, core = place // 2, lax.rem(place, 2)
    me = lax.axis_index("dp")
    slots = layout.shape[2]
    rank = basis_store.shape[2]

    def pair(x):
        return lax.ppermute(x, "seq", [(i, i ^ 1) for i in range(seq_count)])

    def up(x, step):
        moves = [(i, i + 2 * step) for i in range(seq_count) if i + 2 * step < seq_count]
        return lax.ppermute(x, "seq", moves)

    def down(x, step):
        moves = [(i, i - 2 * step) for i in range(seq_count) if i >= 2 * step]
        return lax.ppermute(x, "seq", moves)

    def around(x, step):
        moves = [(i, (i + 2 * step) % seq_count) for i in range(seq_count)]
        return lax.ppermute(x, "seq", moves)

    def across(x, step):
        return lax.ppermute(x, "dp", [(i, i ^ step) for i in range(dp_count)])

    heads = KV_HEADS // CHUNKS
    part = heads * HEAD_DIM

    def packed(chunk):
        columns = slice(chunk * part, (chunk + 1) * part)
        return jnp.concatenate([keys[0][:, columns], values[0][:, columns]], axis=1)

    arrived = []
    for chunk in range(CHUNKS):
        kv = packed(chunk)
        same = [kv]
        for step in range(1, chips):
            if chunk and step == 2:
                kv, arrived[chunk - 1] = lax.optimization_barrier((kv, arrived[chunk - 1]))
            same.append(up(kv, step))
        arrived.append(same)
    beside = [pair(same[0]) for same in arrived]
    table = lists_by_length(layout, place, chips)

    pieces = KV_HEADS
    half = lax.dynamic_slice_in_dim(basis_store[0], core * pieces * HEAD_DIM, pieces * HEAD_DIM, 0)
    owners = lax.dynamic_slice_in_dim(owner, core * pieces, pieces, 0)
    from_where = (owners ^ me)[:, None, None]
    mine = half.reshape(pieces, HEAD_DIM, rank)
    step = 1
    while step < dp_count:
        came = across(mine.reshape(half.shape), step).reshape(mine.shape)
        mine = jnp.where((from_where & step) != 0, came, mine)
        step *= 2
    mine = mine.reshape(half.shape)
    other = pair(mine)

    share = layer_input.shape[2] // (seq_count * dp_count)
    x_pieces = layer_input[0].reshape(BLOCK, chips, 2, dp_count, share)
    x_pieces = jnp.transpose(x_pieces, (3, 0, 2, 1, 4)).reshape(dp_count, BLOCK, seq_count * share)
    x_all = lax.all_to_all(x_pieces, "dp", 0, 0, tiled=True)

    query_grads, grads = [], []
    for chunk in range(CHUNKS):
        if chunk:
            arrived[chunk][1:], grads = lax.optimization_barrier((arrived[chunk][1:], grads))
        kv_parts = arrived[chunk] + [beside[chunk]] + [pair(piece) for piece in arrived[chunk][1:]]
        query_grad, grad = attention(
            table, queries[0], grad_out[0], kv_parts, slots, chunk * heads, heads
        )
        query_grads.append(query_grad)
        grads.append(grad)
    grad_query = jnp.concatenate(query_grads, axis=1)

    keep, send = project(mine, other, grads, chips)
    own, *sends = fold(keep, pair(send), chips)
    total = own
    for step in range(1, chips):
        total = total + down(sends[step - 1], step).astype(f32)
    projected = total.astype(bf16)
    p_parts = [projected] + [across(projected, step) for step in range(1, dp_count)]
    kept, sent = outer(x_all, p_parts)
    own, *sends = deal(kept, pair(sent), chips)
    total = own
    for step in range(1, chips):
        total = total + around(sends[step - 1], step).astype(f32)
    rows = total.astype(bf16)
    lowrank_grad = lay([rows] + [across(rows, step) for step in range(1, dp_count)])
    return (grad_query[None], lowrank_grad)


def solution(mesh):
    in_specs = (
        P("dp", "seq", None),
        P("dp", "seq", None),
        P("dp", "seq", None),
        P("dp", "seq", None),
        P("dp", "seq", None),
        P("dp", None, None),
        P(),
        P(),
    )
    out_specs = (P("dp", "seq", None), P("seq", None))
    return jax.shard_map(local, mesh=mesh, in_specs=in_specs, out_specs=out_specs, check_vma=False)
```

```python
import math
from functools import partial

import jax
import jax.numpy as jnp
from jax import lax
from jax.experimental import pallas as pl
from jax.experimental.pallas import tpu as pltpu
from jax.sharding import PartitionSpec as P

HEADS = 32
KV_HEADS = 4
HEAD_DIM = 128
BLOCK = 128
GROUP = HEADS // KV_HEADS
UNROLL = 4
CHUNKS = 2
VMEM_ATT = 24 * 1024 * 1024
MASKED = -1e30

bf16 = jnp.bfloat16
f32 = jnp.float32
NT = (((1,), (1,)), ((), ()))
NN = (((1,), (0,)), ((), ()))
TN = (((0,), (0,)), ((), ()))


def mm(a, b, dims=NN):
    return lax.dot_general(a, b, dims, preferred_element_type=f32)


def lists_by_length(layout, place, chips):
    slots = layout.shape[2]
    chip, core = place // 2, lax.rem(place, 2)
    lists = lax.dynamic_slice_in_dim(layout, place, 1, 1)[:, 0]
    length = jnp.sum((lists >= 0).astype(jnp.int32), axis=1)
    spots = (chip - lists // 2) + chips * ((lists + core) % 2)
    earlier = jnp.arange(slots, dtype=jnp.int32)[None] < length[:, None] - 1
    spots = jnp.where(earlier, spots, 0)
    within = jnp.arange(HEADS, dtype=jnp.int32) % GROUP
    table = jnp.concatenate([within[:, None], length[:, None], spots[:, : slots - 1]], axis=1)
    table = table.reshape(KV_HEADS, GROUP, slots + 1)
    size = length.reshape(KV_HEADS, GROUP)
    inside = jnp.arange(GROUP, dtype=jnp.int32)
    mine, others = size[:, :, None], size[:, None, :]
    ahead = (others > mine) | ((others == mine) & (inside[None, None, :] < inside[None, :, None]))
    rank = jnp.sum(ahead.astype(jnp.int32), axis=2)
    chosen = rank[:, :, None] == inside[None, None, :]
    ordered = jnp.sum(jnp.where(chosen[..., None], table[:, :, None, :], 0), axis=1)
    return ordered.reshape(-1)


def attention_kernel(table_ref, q_ref, do_ref, *refs, chips, slots, first, heads):
    count = 2 * chips
    kv_refs, refs = refs[:count], refs[count:]
    dq_ref, grads_ref, kbuf, ktbuf, vbuf, dk_acc, dv_acc = refs
    row = slots + 1
    scale = HEAD_DIM ** (-0.5)
    to_exp2 = scale * math.log2(math.e)
    rows = lax.broadcasted_iota(jnp.int32, (BLOCK, BLOCK), 0)
    columns = lax.broadcasted_iota(jnp.int32, (BLOCK, BLOCK), 1)
    causal = rows <= columns

    def one_kv_head(kv_head):
        k_lane = slice(kv_head * HEAD_DIM, (kv_head + 1) * HEAD_DIM)
        v_lane = slice((heads + kv_head) * HEAD_DIM, (heads + kv_head + 1) * HEAD_DIM)
        for index in range(count):
            block = kv_refs[index][:, k_lane]
            kbuf[index] = block
            ktbuf[index] = block.T
            vbuf[index] = kv_refs[index][:, v_lane]
        dk_acc[...] = jnp.zeros_like(dk_acc)
        dv_acc[...] = jnp.zeros_like(dv_acc)

        def heads_step(step, carry):
            base = ((first + kv_head) * GROUP + step * UNROLL) * row
            most = table_ref[base + 1]

            def work(width):
                units = range(UNROLL)
                lanes_in, lanes_out, spots, valid = [], [], [], []
                for unit in units:
                    start = base + unit * row
                    head = table_ref[start]
                    length = table_ref[start + 1]
                    spots.append([0] + [table_ref[start + 1 + slot] for slot in range(1, width)])
                    valid.append([None] + [slot < length for slot in range(1, width)])
                    at_in = ((first + kv_head) * GROUP + head) * HEAD_DIM
                    at_out = (kv_head * GROUP + head) * HEAD_DIM
                    lanes_in.append(pl.ds(pl.multiple_of(at_in, HEAD_DIM), HEAD_DIM))
                    lanes_out.append(pl.ds(pl.multiple_of(at_out, HEAD_DIM), HEAD_DIM))
                qs = [q_ref[:, lanes_in[unit]] for unit in units]
                dos = [do_ref[:, lanes_in[unit]] for unit in units]
                scores, dweights = [], []
                for unit in units:
                    ks = jnp.concatenate([kbuf[spot] for spot in spots[unit]], axis=0)
                    scores.append(mm(ks, qs[unit], NT))
                for unit in units:
                    vs = jnp.concatenate([vbuf[spot] for spot in spots[unit]], axis=0)
                    dweights.append(mm(vs, dos[unit], NT))
                lows, dlows = [], []
                for unit in units:
                    pieces = []
                    for slot in range(width):
                        piece = scores[unit][slot * BLOCK : (slot + 1) * BLOCK] * to_exp2
                        shown = causal if slot == 0 else valid[unit][slot]
                        pieces.append(jnp.where(shown, piece, MASKED))
                    masked = jnp.concatenate(pieces, axis=0)
                    top = jnp.max(masked, axis=0, keepdims=True)
                    raw = jnp.exp2(masked - top)
                    weights = raw * (1.0 / jnp.sum(raw, axis=0, keepdims=True))
                    delta = jnp.sum(weights * dweights[unit], axis=0, keepdims=True)
                    lows.append(weights.astype(bf16))
                    dlows.append((weights * (dweights[unit] - delta)).astype(bf16))
                for unit in units:
                    kt = jnp.concatenate([ktbuf[spot] for spot in spots[unit]], axis=1)
                    dq_ref[:, lanes_out[unit]] = (mm(kt, dlows[unit]) * scale).astype(bf16).T
                dk_acc[0] += mm(
                    jnp.concatenate([dlow[:BLOCK] for dlow in dlows], axis=1),
                    jnp.concatenate(qs, axis=0),
                )
                dv_acc[0] += mm(
                    jnp.concatenate([low[:BLOCK] for low in lows], axis=1),
                    jnp.concatenate(dos, axis=0),
                )
                if width > 1:
                    for unit in units:
                        dk = mm(dlows[unit][BLOCK:], qs[unit])
                        dv = mm(lows[unit][BLOCK:], dos[unit])
                        for slot in range(1, width):
                            part = slice((slot - 1) * BLOCK, slot * BLOCK)
                            dk_acc[spots[unit][slot]] += dk[part]
                            dv_acc[spots[unit][slot]] += dv[part]

            for width in range(1, slots + 1):
                pl.when(most == width)(partial(work, width))
            return carry

        lax.fori_loop(0, GROUP // UNROLL, heads_step, 0)
        for index in range(count):
            at = slice(index * BLOCK, (index + 1) * BLOCK)
            grads_ref[at, k_lane] = (dk_acc[index] * scale).astype(bf16)
            grads_ref[at, v_lane] = dv_acc[index].astype(bf16)

    for kv_head in range(heads):
        one_kv_head(kv_head)


def attention(table, queries, grads, kv_parts, slots, first, heads):
    count = len(kv_parts)
    body = partial(attention_kernel, chips=count // 2, slots=slots, first=first, heads=heads)
    whole = pl.BlockSpec(memory_space=pltpu.VMEM)
    pairs = heads * GROUP * 3
    return pl.pallas_call(
        body,
        in_specs=[pl.BlockSpec(memory_space=pltpu.SMEM)] + [whole] * (2 + count),
        out_specs=[whole, whole],
        out_shape=[
            jax.ShapeDtypeStruct((BLOCK, heads * GROUP * HEAD_DIM), bf16),
            jax.ShapeDtypeStruct((count * BLOCK, 2 * heads * HEAD_DIM), bf16),
        ],
        scratch_shapes=[
            pltpu.VMEM((count, BLOCK, HEAD_DIM), bf16),
            pltpu.VMEM((count, HEAD_DIM, BLOCK), bf16),
            pltpu.VMEM((count, BLOCK, HEAD_DIM), bf16),
            pltpu.VMEM((count, BLOCK, HEAD_DIM), f32),
            pltpu.VMEM((count, BLOCK, HEAD_DIM), f32),
        ],
        compiler_params=pltpu.CompilerParams(vmem_limit_bytes=VMEM_ATT),
        cost_estimate=pl.CostEstimate(
            flops=pairs * 100 * BLOCK**3, bytes_accessed=4 << 20, transcendentals=pairs * BLOCK**2
        ),
        name="attention_backward",
    )(table, queries, grads, *kv_parts)

def project_kernel(mine_ref, other_ref, *refs, chips, chunks):
    grads_refs, refs = refs[:chunks], refs[chunks:]
    keep_ref, send_ref, basis = refs
    half = mine_ref.shape[0]
    core = lax.rem(lax.axis_index("seq"), 2)

    @pl.when(core == 0)
    def _():
        basis[:half] = mine_ref[...]
        basis[half:] = other_ref[...]

    @pl.when(core == 1)
    def _():
        basis[:half] = other_ref[...]
        basis[half:] = mine_ref[...]

    chosen = basis[...]
    part = grads_refs[0].shape[1] // 2
    tall = min(chips, 4) * BLOCK

    def product(start):
        rows = slice(start, start + tall)
        keys = [ref[rows, :part] for ref in grads_refs]
        values = [ref[rows, part:] for ref in grads_refs]
        return mm(jnp.concatenate(keys + values, axis=1), chosen)

    for start in range(0, chips * BLOCK, tall):
        send_ref[start : start + tall] = product(chips * BLOCK + start).astype(bf16)
        keep_ref[start : start + tall] = product(start)


def project(mine, other, grads, chips):
    rank = mine.shape[1]
    return pl.pallas_call(
        partial(project_kernel, chips=chips, chunks=len(grads)),
        out_shape=[
            jax.ShapeDtypeStruct((chips * BLOCK, rank), f32),
            jax.ShapeDtypeStruct((chips * BLOCK, rank), bf16),
        ],
        scratch_shapes=[pltpu.VMEM((2 * mine.shape[0], rank), bf16)],
        compiler_params=pltpu.CompilerParams(vmem_limit_bytes=32 * 1024 * 1024),
        name="project",
    )(mine, other, *grads)


def fold_kernel(keep_ref, came_ref, own_ref, *send_refs):
    own_ref[...] = keep_ref[:BLOCK] + came_ref[:BLOCK].astype(f32)
    for index, send_ref in enumerate(send_refs):
        rows = slice((index + 1) * BLOCK, (index + 2) * BLOCK)
        send_ref[...] = (keep_ref[rows] + came_ref[rows].astype(f32)).astype(bf16)


def fold(keep, came, chips):
    rank = keep.shape[1]
    return pl.pallas_call(
        fold_kernel,
        out_shape=[jax.ShapeDtypeStruct((BLOCK, rank), f32)]
        + [jax.ShapeDtypeStruct((BLOCK, rank), bf16)] * (chips - 1),
        compiler_params=pltpu.CompilerParams(vmem_limit_bytes=32 * 1024 * 1024),
        name="fold_parts",
    )(keep, came)


def outer_kernel(x_ref, *refs, dp_count):
    p_refs, refs = refs[:dp_count], refs[dp_count:]
    keep_ref, send_ref = refs
    core = lax.rem(lax.axis_index("seq"), 2)
    me = lax.axis_index("dp")
    half = keep_ref.shape[0]
    projected = jnp.concatenate([ref[...] for ref in p_refs], axis=0)

    def product(which):
        columns = pl.ds(pl.multiple_of(which * half, half), half)
        inputs = [x_ref[jnp.bitwise_xor(me, step), :, columns] for step in range(dp_count)]
        return mm(jnp.concatenate(inputs, axis=0), projected, TN)

    send_ref[...] = product(1 - core).astype(bf16)
    keep_ref[...] = product(core)


def outer(x_all, p_parts):
    features = x_all.shape[2]
    rank = p_parts[0].shape[1]
    return pl.pallas_call(
        partial(outer_kernel, dp_count=len(p_parts)),
        out_shape=[
            jax.ShapeDtypeStruct((features // 2, rank), f32),
            jax.ShapeDtypeStruct((features // 2, rank), bf16),
        ],
        compiler_params=pltpu.CompilerParams(vmem_limit_bytes=32 * 1024 * 1024),
        name="outer_product",
    )(x_all, *p_parts)


def deal_kernel(keep_ref, came_ref, own_ref, *refs):
    send_refs, total = refs[:-1], refs[-1]
    chips = len(send_refs) + 1
    chip = lax.axis_index("seq") // 2
    share = own_ref.shape[0]
    total[...] = keep_ref[...] + came_ref[...].astype(f32)

    def rows(step):
        return pl.ds(pl.multiple_of(lax.rem(chip + step, chips) * share, share), share)

    own_ref[...] = total[rows(0)]
    for step, send_ref in enumerate(send_refs, 1):
        send_ref[...] = total[rows(step)].astype(bf16)


def deal(keep, came, chips):
    share, rank = keep.shape[0] // chips, keep.shape[1]
    return pl.pallas_call(
        deal_kernel,
        out_shape=[jax.ShapeDtypeStruct((share, rank), f32)]
        + [jax.ShapeDtypeStruct((share, rank), bf16)] * (chips - 1),
        scratch_shapes=[pltpu.VMEM(keep.shape, f32)],
        compiler_params=pltpu.CompilerParams(vmem_limit_bytes=32 * 1024 * 1024),
        name="deal_rows",
    )(keep, came)


def lay_kernel(*refs):
    part_refs, out_ref = refs[:-1], refs[-1]
    me = lax.axis_index("dp")
    share = part_refs[0].shape[0]
    for step, part_ref in enumerate(part_refs):
        at = pl.multiple_of(jnp.bitwise_xor(me, step) * share, share)
        out_ref[pl.ds(at, share)] = part_ref[...].astype(f32) * (1.0 / len(part_refs))


def lay(parts):
    share, rank = parts[0].shape
    return pl.pallas_call(
        lay_kernel,
        out_shape=jax.ShapeDtypeStruct((share * len(parts), rank), f32),
        compiler_params=pltpu.CompilerParams(vmem_limit_bytes=32 * 1024 * 1024),
        name="lay_rows",
    )(*parts)


def local(queries, keys, values, grad_out, layer_input, basis_store, owner, layout):
    seq_count = lax.axis_size("seq")
    dp_count = lax.axis_size("dp")
    chips = seq_count // 2
    place = lax.axis_index("seq")
    chip, core = place // 2, lax.rem(place, 2)
    me = lax.axis_index("dp")
    slots = layout.shape[2]
    rank = basis_store.shape[2]

    def pair(x):
        return lax.ppermute(x, "seq", [(i, i ^ 1) for i in range(seq_count)])

    def around(x, step):
        moves = [(i, (i + 2 * step) % seq_count) for i in range(seq_count)]
        return lax.ppermute(x, "seq", moves)

    def up(x, step):
        return around(x, step)

    def down(x, step):
        return around(x, -step)

    def across(x, step):
        return lax.ppermute(x, "dp", [(i, i ^ step) for i in range(dp_count)])

    heads = KV_HEADS // CHUNKS
    part = heads * HEAD_DIM

    def packed(chunk):
        columns = slice(chunk * part, (chunk + 1) * part)
        return jnp.concatenate([keys[0][:, columns], values[0][:, columns]], axis=1)

    arrived = []
    for chunk in range(CHUNKS):
        kv = packed(chunk)
        same = [kv]
        for step in range(1, chips):
            if chunk and step == 2:
                kv, arrived[chunk - 1] = lax.optimization_barrier((kv, arrived[chunk - 1]))
            same.append(up(kv, step))
        arrived.append(same)
    beside = [pair(same[0]) for same in arrived]
    table = lists_by_length(layout, place, chips)

    pieces = KV_HEADS
    half = lax.dynamic_slice_in_dim(basis_store[0], core * pieces * HEAD_DIM, pieces * HEAD_DIM, 0)
    owners = lax.dynamic_slice_in_dim(owner, core * pieces, pieces, 0)
    from_where = (owners ^ me)[:, None, None]
    mine = half.reshape(pieces, HEAD_DIM, rank)
    step = 1
    while step < dp_count:
        came = across(mine.reshape(half.shape), step).reshape(mine.shape)
        mine = jnp.where((from_where & step) != 0, came, mine)
        step *= 2
    mine = mine.reshape(half.shape)
    other = pair(mine)

    share = layer_input.shape[2] // (seq_count * dp_count)
    x_pieces = layer_input[0].reshape(BLOCK, chips, 2, dp_count, share)
    x_pieces = jnp.transpose(x_pieces, (3, 0, 2, 1, 4)).reshape(dp_count, BLOCK, seq_count * share)
    x_all = lax.all_to_all(x_pieces, "dp", 0, 0, tiled=True)

    query_grads, grads = [], []
    for chunk in range(CHUNKS):
        if chunk:
            arrived[chunk][1:], grads = lax.optimization_barrier((arrived[chunk][1:], grads))
        kv_parts = arrived[chunk] + [beside[chunk]] + [pair(piece) for piece in arrived[chunk][1:]]
        query_grad, grad = attention(
            table, queries[0], grad_out[0], kv_parts, slots, chunk * heads, heads
        )
        query_grads.append(query_grad)
        grads.append(grad)
    grad_query = jnp.concatenate(query_grads, axis=1)

    keep, send = project(mine, other, grads, chips)
    own, *sends = fold(keep, pair(send), chips)
    total = own
    for step in range(1, chips):
        total = total + down(sends[step - 1], step).astype(f32)
    projected = total.astype(bf16)
    p_parts = [projected] + [across(projected, step) for step in range(1, dp_count)]
    kept, sent = outer(x_all, p_parts)
    own, *sends = deal(kept, pair(sent), chips)
    total = own
    for step in range(1, chips):
        total = total + around(sends[step - 1], step).astype(f32)
    rows = total.astype(bf16)
    lowrank_grad = lay([rows] + [across(rows, step) for step in range(1, dp_count)])
    return (grad_query[None], lowrank_grad)


def solution(mesh):
    in_specs = (
        P("dp", "seq", None),
        P("dp", "seq", None),
        P("dp", "seq", None),
        P("dp", "seq", None),
        P("dp", "seq", None),
        P("dp", None, None),
        P(),
        P(),
    )
    out_specs = (P("dp", "seq", None), P("seq", None))
    return jax.shard_map(local, mesh=mesh, in_specs=in_specs, out_specs=out_specs, check_vma=False)
```

```python
import math
from functools import partial

import jax
import jax.numpy as jnp
from jax import lax
from jax.experimental import pallas as pl
from jax.experimental.pallas import tpu as pltpu
from jax.sharding import PartitionSpec as P

HEADS = 32
KV_HEADS = 4
HEAD_DIM = 128
BLOCK = 128
GROUP = HEADS // KV_HEADS
UNROLL = 4
CHUNKS = 2
VMEM_ATT = 24 * 1024 * 1024
MASKED = -1e30

bf16 = jnp.bfloat16
f32 = jnp.float32
NT = (((1,), (1,)), ((), ()))
NN = (((1,), (0,)), ((), ()))
TN = (((0,), (0,)), ((), ()))


def mm(a, b, dims=NN):
    return lax.dot_general(a, b, dims, preferred_element_type=f32)


def lists_by_length(layout, place, chips):
    slots = layout.shape[2]
    chip, core = place // 2, lax.rem(place, 2)
    lists = lax.dynamic_slice_in_dim(layout, place, 1, 1)[:, 0]
    length = jnp.sum((lists >= 0).astype(jnp.int32), axis=1)
    spots = (chip - lists // 2) + chips * ((lists + core) % 2)
    earlier = jnp.arange(slots, dtype=jnp.int32)[None] < length[:, None] - 1
    spots = jnp.where(earlier, spots, 0)
    within = jnp.arange(HEADS, dtype=jnp.int32) % GROUP
    table = jnp.concatenate([within[:, None], length[:, None], spots[:, : slots - 1]], axis=1)
    table = table.reshape(KV_HEADS, GROUP, slots + 1)
    size = length.reshape(KV_HEADS, GROUP)
    inside = jnp.arange(GROUP, dtype=jnp.int32)
    mine, others = size[:, :, None], size[:, None, :]
    ahead = (others > mine) | ((others == mine) & (inside[None, None, :] < inside[None, :, None]))
    rank = jnp.sum(ahead.astype(jnp.int32), axis=2)
    chosen = rank[:, :, None] == inside[None, None, :]
    ordered = jnp.sum(jnp.where(chosen[..., None], table[:, :, None, :], 0), axis=1)
    return ordered.reshape(-1)


def attention_kernel(table_ref, q_ref, do_ref, *refs, chips, slots, first, heads):
    count = 2 * chips
    kv_refs, refs = refs[:count], refs[count:]
    dq_ref, grads_ref, kbuf, ktbuf, vbuf, dk_acc, dv_acc = refs
    row = slots + 1
    scale = HEAD_DIM ** (-0.5)
    to_exp2 = scale * math.log2(math.e)
    rows = lax.broadcasted_iota(jnp.int32, (BLOCK, BLOCK), 0)
    columns = lax.broadcasted_iota(jnp.int32, (BLOCK, BLOCK), 1)
    causal = rows <= columns

    def one_kv_head(kv_head):
        k_lane = slice(kv_head * HEAD_DIM, (kv_head + 1) * HEAD_DIM)
        v_lane = slice((heads + kv_head) * HEAD_DIM, (heads + kv_head + 1) * HEAD_DIM)
        for index in range(count):
            block = kv_refs[index][:, k_lane]
            kbuf[index] = block
            ktbuf[index] = block.T
            vbuf[index] = kv_refs[index][:, v_lane]
        dk_acc[...] = jnp.zeros_like(dk_acc)
        dv_acc[...] = jnp.zeros_like(dv_acc)

        def heads_step(step, carry):
            base = ((first + kv_head) * GROUP + step * UNROLL) * row
            most = table_ref[base + 1]

            def work(width):
                units = range(UNROLL)
                lanes_in, lanes_out, spots, valid = [], [], [], []
                for unit in units:
                    start = base + unit * row
                    head = table_ref[start]
                    length = table_ref[start + 1]
                    spots.append([0] + [table_ref[start + 1 + slot] for slot in range(1, width)])
                    valid.append([None] + [slot < length for slot in range(1, width)])
                    at_in = ((first + kv_head) * GROUP + head) * HEAD_DIM
                    at_out = (kv_head * GROUP + head) * HEAD_DIM
                    lanes_in.append(pl.ds(pl.multiple_of(at_in, HEAD_DIM), HEAD_DIM))
                    lanes_out.append(pl.ds(pl.multiple_of(at_out, HEAD_DIM), HEAD_DIM))
                qs = [q_ref[:, lanes_in[unit]] for unit in units]
                dos = [do_ref[:, lanes_in[unit]] for unit in units]
                scores, dweights = [], []
                for unit in units:
                    ks = jnp.concatenate([kbuf[spot] for spot in spots[unit]], axis=0)
                    scores.append(mm(ks, qs[unit], NT))
                for unit in units:
                    vs = jnp.concatenate([vbuf[spot] for spot in spots[unit]], axis=0)
                    dweights.append(mm(vs, dos[unit], NT))
                lows, dlows = [], []
                for unit in units:
                    pieces = []
                    for slot in range(width):
                        piece = scores[unit][slot * BLOCK : (slot + 1) * BLOCK] * to_exp2
                        shown = causal if slot == 0 else valid[unit][slot]
                        pieces.append(jnp.where(shown, piece, MASKED))
                    masked = jnp.concatenate(pieces, axis=0)
                    top = jnp.max(masked, axis=0, keepdims=True)
                    raw = jnp.exp2(masked - top)
                    weights = raw * (1.0 / jnp.sum(raw, axis=0, keepdims=True))
                    delta = jnp.sum(weights * dweights[unit], axis=0, keepdims=True)
                    lows.append(weights.astype(bf16))
                    dlows.append((weights * (dweights[unit] - delta)).astype(bf16))
                for unit in units:
                    kt = jnp.concatenate([ktbuf[spot] for spot in spots[unit]], axis=1)
                    dq_ref[:, lanes_out[unit]] = (mm(kt, dlows[unit]) * scale).astype(bf16).T
                dk_acc[0] += mm(
                    jnp.concatenate([dlow[:BLOCK] for dlow in dlows], axis=1),
                    jnp.concatenate(qs, axis=0),
                )
                dv_acc[0] += mm(
                    jnp.concatenate([low[:BLOCK] for low in lows], axis=1),
                    jnp.concatenate(dos, axis=0),
                )
                if width > 1:
                    for unit in units:
                        dk = mm(dlows[unit][BLOCK:], qs[unit])
                        dv = mm(lows[unit][BLOCK:], dos[unit])
                        for slot in range(1, width):
                            part = slice((slot - 1) * BLOCK, slot * BLOCK)
                            dk_acc[spots[unit][slot]] += dk[part]
                            dv_acc[spots[unit][slot]] += dv[part]

            for width in range(1, slots + 1):
                pl.when(most == width)(partial(work, width))
            return carry

        lax.fori_loop(0, GROUP // UNROLL, heads_step, 0)
        for index in range(count):
            at = slice(index * BLOCK, (index + 1) * BLOCK)
            grads_ref[at, k_lane] = (dk_acc[index] * scale).astype(bf16)
            grads_ref[at, v_lane] = dv_acc[index].astype(bf16)

    for kv_head in range(heads):
        one_kv_head(kv_head)


def attention(table, queries, grads, kv_parts, slots, first, heads):
    count = len(kv_parts)
    body = partial(attention_kernel, chips=count // 2, slots=slots, first=first, heads=heads)
    whole = pl.BlockSpec(memory_space=pltpu.VMEM)
    pairs = heads * GROUP * 3
    return pl.pallas_call(
        body,
        in_specs=[pl.BlockSpec(memory_space=pltpu.SMEM)] + [whole] * (2 + count),
        out_specs=[whole, whole],
        out_shape=[
            jax.ShapeDtypeStruct((BLOCK, heads * GROUP * HEAD_DIM), bf16),
            jax.ShapeDtypeStruct((count * BLOCK, 2 * heads * HEAD_DIM), bf16),
        ],
        scratch_shapes=[
            pltpu.VMEM((count, BLOCK, HEAD_DIM), bf16),
            pltpu.VMEM((count, HEAD_DIM, BLOCK), bf16),
            pltpu.VMEM((count, BLOCK, HEAD_DIM), bf16),
            pltpu.VMEM((count, BLOCK, HEAD_DIM), f32),
            pltpu.VMEM((count, BLOCK, HEAD_DIM), f32),
        ],
        compiler_params=pltpu.CompilerParams(vmem_limit_bytes=VMEM_ATT),
        cost_estimate=pl.CostEstimate(
            flops=pairs * 100 * BLOCK**3, bytes_accessed=4 << 20, transcendentals=pairs * BLOCK**2
        ),
        name="attention_backward",
    )(table, queries, grads, *kv_parts)

def project_kernel(mine_ref, other_ref, *refs, chips, chunks):
    grads_refs, refs = refs[:chunks], refs[chunks:]
    keep_ref, send_ref, basis = refs
    half = mine_ref.shape[0]
    core = lax.rem(lax.axis_index("seq"), 2)

    @pl.when(core == 0)
    def _():
        basis[:half] = mine_ref[...]
        basis[half:] = other_ref[...]

    @pl.when(core == 1)
    def _():
        basis[:half] = other_ref[...]
        basis[half:] = mine_ref[...]

    chosen = basis[...]
    part = grads_refs[0].shape[1] // 2
    tall = min(chips, 4) * BLOCK

    def product(start):
        rows = slice(start, start + tall)
        keys = [ref[rows, :part] for ref in grads_refs]
        values = [ref[rows, part:] for ref in grads_refs]
        return mm(jnp.concatenate(keys + values, axis=1), chosen)

    for start in range(0, chips * BLOCK, tall):
        send_ref[start : start + tall] = product(chips * BLOCK + start).astype(bf16)
        keep_ref[start : start + tall] = product(start)


def project(mine, other, grads, chips):
    rank = mine.shape[1]
    return pl.pallas_call(
        partial(project_kernel, chips=chips, chunks=len(grads)),
        out_shape=[
            jax.ShapeDtypeStruct((chips * BLOCK, rank), f32),
            jax.ShapeDtypeStruct((chips * BLOCK, rank), bf16),
        ],
        scratch_shapes=[pltpu.VMEM((2 * mine.shape[0], rank), bf16)],
        compiler_params=pltpu.CompilerParams(vmem_limit_bytes=32 * 1024 * 1024),
        name="project",
    )(mine, other, *grads)


def fold_kernel(keep_ref, came_ref, own_ref, *send_refs):
    own_ref[...] = keep_ref[:BLOCK] + came_ref[:BLOCK].astype(f32)
    for index, send_ref in enumerate(send_refs):
        rows = slice((index + 1) * BLOCK, (index + 2) * BLOCK)
        send_ref[...] = (keep_ref[rows] + came_ref[rows].astype(f32)).astype(bf16)


def fold(keep, came, chips):
    rank = keep.shape[1]
    return pl.pallas_call(
        fold_kernel,
        out_shape=[jax.ShapeDtypeStruct((BLOCK, rank), f32)]
        + [jax.ShapeDtypeStruct((BLOCK, rank), bf16)] * (chips - 1),
        compiler_params=pltpu.CompilerParams(vmem_limit_bytes=32 * 1024 * 1024),
        name="fold_parts",
    )(keep, came)


def outer_kernel(x_ref, *refs, dp_count):
    p_refs, refs = refs[:dp_count], refs[dp_count:]
    keep_ref, send_ref = refs
    core = lax.rem(lax.axis_index("seq"), 2)
    me = lax.axis_index("dp")
    half = keep_ref.shape[0]
    projected = jnp.concatenate([ref[...] for ref in p_refs], axis=0)

    def product(which):
        columns = pl.ds(pl.multiple_of(which * half, half), half)
        inputs = [x_ref[jnp.bitwise_xor(me, step), :, columns] for step in range(dp_count)]
        return mm(jnp.concatenate(inputs, axis=0), projected, TN)

    send_ref[...] = product(1 - core).astype(bf16)
    keep_ref[...] = product(core)


def outer(x_all, p_parts):
    features = x_all.shape[2]
    rank = p_parts[0].shape[1]
    return pl.pallas_call(
        partial(outer_kernel, dp_count=len(p_parts)),
        out_shape=[
            jax.ShapeDtypeStruct((features // 2, rank), f32),
            jax.ShapeDtypeStruct((features // 2, rank), bf16),
        ],
        compiler_params=pltpu.CompilerParams(vmem_limit_bytes=32 * 1024 * 1024),
        name="outer_product",
    )(x_all, *p_parts)


def deal_kernel(keep_ref, came_ref, own_ref, *refs):
    send_refs, total = refs[:-1], refs[-1]
    chips = len(send_refs) + 1
    chip = lax.axis_index("seq") // 2
    share = own_ref.shape[0]
    total[...] = keep_ref[...] + came_ref[...].astype(f32)

    def rows(step):
        return pl.ds(pl.multiple_of(lax.rem(chip + step, chips) * share, share), share)

    own_ref[...] = total[rows(0)]
    for step, send_ref in enumerate(send_refs, 1):
        send_ref[...] = total[rows(step)].astype(bf16)


def deal(keep, came, chips):
    share, rank = keep.shape[0] // chips, keep.shape[1]
    return pl.pallas_call(
        deal_kernel,
        out_shape=[jax.ShapeDtypeStruct((share, rank), f32)]
        + [jax.ShapeDtypeStruct((share, rank), bf16)] * (chips - 1),
        scratch_shapes=[pltpu.VMEM(keep.shape, f32)],
        compiler_params=pltpu.CompilerParams(vmem_limit_bytes=32 * 1024 * 1024),
        name="deal_rows",
    )(keep, came)


def lay_kernel(*refs):
    part_refs, out_ref = refs[:-1], refs[-1]
    me = lax.axis_index("dp")
    share = part_refs[0].shape[0]
    for step, part_ref in enumerate(part_refs):
        at = pl.multiple_of(jnp.bitwise_xor(me, step) * share, share)
        out_ref[pl.ds(at, share)] = part_ref[...].astype(f32) * (1.0 / len(part_refs))


def lay(parts):
    share, rank = parts[0].shape
    return pl.pallas_call(
        lay_kernel,
        out_shape=jax.ShapeDtypeStruct((share * len(parts), rank), f32),
        compiler_params=pltpu.CompilerParams(vmem_limit_bytes=32 * 1024 * 1024),
        name="lay_rows",
    )(*parts)


def split_kernel(x_ref, out_ref, *, chips):
    dp_count, _, width = out_ref.shape
    share = width // (2 * chips)
    for place in range(2 * chips):
        to = (place % 2 * chips + place // 2) * share
        for group in range(dp_count):
            at = (place * dp_count + group) * share
            out_ref[group, :, to : to + share] = x_ref[:, at : at + share]


def split_input(x, chips, dp_count):
    features = x.shape[1]
    share = features // (2 * chips * dp_count)
    if share % 128 != 0:
        pieces = jnp.transpose(x.reshape(BLOCK, chips, 2, dp_count, share), (3, 0, 2, 1, 4))
        return pieces.reshape(dp_count, BLOCK, features // dp_count)
    return pl.pallas_call(
        partial(split_kernel, chips=chips),
        out_shape=jax.ShapeDtypeStruct((dp_count, BLOCK, features // dp_count), bf16),
        compiler_params=pltpu.CompilerParams(vmem_limit_bytes=16 * 1024 * 1024),
        name="split_input",
    )(x)


def local(queries, keys, values, grad_out, layer_input, basis_store, owner, layout):
    seq_count = lax.axis_size("seq")
    dp_count = lax.axis_size("dp")
    chips = seq_count // 2
    place = lax.axis_index("seq")
    chip, core = place // 2, lax.rem(place, 2)
    me = lax.axis_index("dp")
    slots = layout.shape[2]
    rank = basis_store.shape[2]

    def pair(x):
        return lax.ppermute(x, "seq", [(i, i ^ 1) for i in range(seq_count)])

    def around(x, step):
        moves = [(i, (i + 2 * step) % seq_count) for i in range(seq_count)]
        return lax.ppermute(x, "seq", moves)

    def up(x, step):
        return around(x, step)

    def down(x, step):
        return around(x, -step)

    def across(x, step):
        return lax.ppermute(x, "dp", [(i, i ^ step) for i in range(dp_count)])

    heads = KV_HEADS // CHUNKS
    part = heads * HEAD_DIM

    def packed(chunk):
        columns = slice(chunk * part, (chunk + 1) * part)
        return jnp.concatenate([keys[0][:, columns], values[0][:, columns]], axis=1)

    arrived = []
    for chunk in range(CHUNKS):
        kv = packed(chunk)
        same = [kv]
        for step in range(1, chips):
            if chunk and step == 3:
                kv, arrived[chunk - 1] = lax.optimization_barrier((kv, arrived[chunk - 1]))
            same.append(up(kv, step))
        arrived.append(same)
    beside = [pair(same[0]) for same in arrived]
    table = lists_by_length(layout, place, chips)

    pieces = KV_HEADS
    half = lax.dynamic_slice_in_dim(basis_store[0], core * pieces * HEAD_DIM, pieces * HEAD_DIM, 0)
    owners = lax.dynamic_slice_in_dim(owner, core * pieces, pieces, 0)
    from_where = (owners ^ me)[:, None, None]
    mine = half.reshape(pieces, HEAD_DIM, rank)
    step = 1
    while step < dp_count:
        came = across(mine.reshape(half.shape), step).reshape(mine.shape)
        mine = jnp.where((from_where & step) != 0, came, mine)
        step *= 2
    mine = mine.reshape(half.shape)
    other = pair(mine)

    x_pieces = split_input(layer_input[0], chips, dp_count)
    x_all = lax.all_to_all(x_pieces, "dp", 0, 0, tiled=True)

    query_grads, grads = [], []
    for chunk in range(CHUNKS):
        if chunk:
            arrived[chunk][1:], grads = lax.optimization_barrier((arrived[chunk][1:], grads))
        kv_parts = arrived[chunk] + [beside[chunk]] + [pair(piece) for piece in arrived[chunk][1:]]
        query_grad, grad = attention(
            table, queries[0], grad_out[0], kv_parts, slots, chunk * heads, heads
        )
        query_grads.append(query_grad)
        grads.append(grad)
    grad_query = jnp.concatenate(query_grads, axis=1)

    keep, send = project(mine, other, grads, chips)
    own, *sends = fold(keep, pair(send), chips)
    total = own
    for step in range(1, chips):
        total = total + down(sends[step - 1], step).astype(f32)
    projected = total.astype(bf16)
    p_parts = [projected] + [across(projected, step) for step in range(1, dp_count)]
    kept, sent = outer(x_all, p_parts)
    own, *sends = deal(kept, pair(sent), chips)
    total = own
    for step in range(1, chips):
        total = total + around(sends[step - 1], step).astype(f32)
    rows = total.astype(bf16)
    lowrank_grad = lay([rows] + [across(rows, step) for step in range(1, dp_count)])
    return (grad_query[None], lowrank_grad)


def solution(mesh):
    in_specs = (
        P("dp", "seq", None),
        P("dp", "seq", None),
        P("dp", "seq", None),
        P("dp", "seq", None),
        P("dp", "seq", None),
        P("dp", None, None),
        P(),
        P(),
    )
    out_specs = (P("dp", "seq", None), P("seq", None))
    return jax.shard_map(local, mesh=mesh, in_specs=in_specs, out_specs=out_specs, check_vma=False)
```

```python
import math
from functools import partial

import jax
import jax.numpy as jnp
from jax import lax
from jax.experimental import pallas as pl
from jax.experimental.pallas import tpu as pltpu
from jax.sharding import PartitionSpec as P

HEADS = 32
KV_HEADS = 4
HEAD_DIM = 128
BLOCK = 128
GROUP = HEADS // KV_HEADS
UNROLL = 4
CHUNKS = 2
VMEM_ATT = 24 * 1024 * 1024
MASKED = -1e30

bf16 = jnp.bfloat16
f32 = jnp.float32
NT = (((1,), (1,)), ((), ()))
NN = (((1,), (0,)), ((), ()))
TN = (((0,), (0,)), ((), ()))


def mm(a, b, dims=NN):
    return lax.dot_general(a, b, dims, preferred_element_type=f32)


def lists_by_length(layout, place, chips):
    slots = layout.shape[2]
    chip, core = place // 2, lax.rem(place, 2)
    lists = lax.dynamic_slice_in_dim(layout, place, 1, 1)[:, 0]
    length = jnp.sum((lists >= 0).astype(jnp.int32), axis=1)
    spots = (chip - lists // 2) + chips * ((lists + core) % 2)
    earlier = jnp.arange(slots, dtype=jnp.int32)[None] < length[:, None] - 1
    spots = jnp.where(earlier, spots, 0)
    within = jnp.arange(HEADS, dtype=jnp.int32) % GROUP
    table = jnp.concatenate([within[:, None], length[:, None], spots[:, : slots - 1]], axis=1)
    table = table.reshape(KV_HEADS, GROUP, slots + 1)
    size = length.reshape(KV_HEADS, GROUP)
    inside = jnp.arange(GROUP, dtype=jnp.int32)
    mine, others = size[:, :, None], size[:, None, :]
    ahead = (others > mine) | ((others == mine) & (inside[None, None, :] < inside[None, :, None]))
    rank = jnp.sum(ahead.astype(jnp.int32), axis=2)
    chosen = rank[:, :, None] == inside[None, None, :]
    ordered = jnp.sum(jnp.where(chosen[..., None], table[:, :, None, :], 0), axis=1)
    return ordered.reshape(-1)


def attention_kernel(table_ref, q_ref, do_ref, *refs, chips, slots, first, heads):
    count = 2 * chips
    kv_refs, refs = refs[:count], refs[count:]
    dq_ref, grads_ref, kbuf, ktbuf, vbuf, dk_acc, dv_acc = refs
    row = slots + 1
    scale = HEAD_DIM ** (-0.5)
    to_exp2 = scale * math.log2(math.e)
    rows = lax.broadcasted_iota(jnp.int32, (BLOCK, BLOCK), 0)
    columns = lax.broadcasted_iota(jnp.int32, (BLOCK, BLOCK), 1)
    causal = rows <= columns

    def one_kv_head(kv_head):
        k_lane = slice(kv_head * HEAD_DIM, (kv_head + 1) * HEAD_DIM)
        v_lane = slice((heads + kv_head) * HEAD_DIM, (heads + kv_head + 1) * HEAD_DIM)
        for index in range(count):
            block = kv_refs[index][:, k_lane]
            kbuf[index] = block
            ktbuf[index] = block.T
            vbuf[index] = kv_refs[index][:, v_lane]
        dk_acc[...] = jnp.zeros_like(dk_acc)
        dv_acc[...] = jnp.zeros_like(dv_acc)

        def heads_step(step, carry):
            base = ((first + kv_head) * GROUP + step * UNROLL) * row
            most = table_ref[base + 1]

            def work(width):
                units = range(UNROLL)
                lanes_in, lanes_out, spots, valid = [], [], [], []
                for unit in units:
                    start = base + unit * row
                    head = table_ref[start]
                    length = table_ref[start + 1]
                    spots.append([0] + [table_ref[start + 1 + slot] for slot in range(1, width)])
                    valid.append([None] + [slot < length for slot in range(1, width)])
                    at_in = ((first + kv_head) * GROUP + head) * HEAD_DIM
                    at_out = (kv_head * GROUP + head) * HEAD_DIM
                    lanes_in.append(pl.ds(pl.multiple_of(at_in, HEAD_DIM), HEAD_DIM))
                    lanes_out.append(pl.ds(pl.multiple_of(at_out, HEAD_DIM), HEAD_DIM))
                qs = [q_ref[:, lanes_in[unit]] for unit in units]
                dos = [do_ref[:, lanes_in[unit]] for unit in units]
                scores, dweights = [], []
                for unit in units:
                    ks = jnp.concatenate([kbuf[spot] for spot in spots[unit]], axis=0)
                    scores.append(mm(ks, qs[unit], NT))
                for unit in units:
                    vs = jnp.concatenate([vbuf[spot] for spot in spots[unit]], axis=0)
                    dweights.append(mm(vs, dos[unit], NT))
                lows, dlows = [], []
                for unit in units:
                    pieces = []
                    for slot in range(width):
                        piece = scores[unit][slot * BLOCK : (slot + 1) * BLOCK] * to_exp2
                        shown = causal if slot == 0 else valid[unit][slot]
                        pieces.append(jnp.where(shown, piece, MASKED))
                    masked = jnp.concatenate(pieces, axis=0)
                    top = jnp.max(masked, axis=0, keepdims=True)
                    raw = jnp.exp2(masked - top)
                    weights = raw * (1.0 / jnp.sum(raw, axis=0, keepdims=True))
                    delta = jnp.sum(weights * dweights[unit], axis=0, keepdims=True)
                    lows.append(weights.astype(bf16))
                    dlows.append((weights * (dweights[unit] - delta)).astype(bf16))
                for unit in units:
                    kt = jnp.concatenate([ktbuf[spot] for spot in spots[unit]], axis=1)
                    dq_ref[:, lanes_out[unit]] = (mm(kt, dlows[unit]) * scale).astype(bf16).T
                dk_acc[0] += mm(
                    jnp.concatenate([dlow[:BLOCK] for dlow in dlows], axis=1),
                    jnp.concatenate(qs, axis=0),
                )
                dv_acc[0] += mm(
                    jnp.concatenate([low[:BLOCK] for low in lows], axis=1),
                    jnp.concatenate(dos, axis=0),
                )
                if width > 1:
                    for unit in units:
                        dk = mm(dlows[unit][BLOCK:], qs[unit])
                        dv = mm(lows[unit][BLOCK:], dos[unit])
                        for slot in range(1, width):
                            part = slice((slot - 1) * BLOCK, slot * BLOCK)
                            dk_acc[spots[unit][slot]] += dk[part]
                            dv_acc[spots[unit][slot]] += dv[part]

            for width in range(1, slots + 1):
                pl.when(most == width)(partial(work, width))
            return carry

        lax.fori_loop(0, GROUP // UNROLL, heads_step, 0)
        for index in range(count):
            at = slice(index * BLOCK, (index + 1) * BLOCK)
            grads_ref[at, k_lane] = (dk_acc[index] * scale).astype(bf16)
            grads_ref[at, v_lane] = dv_acc[index].astype(bf16)

    for kv_head in range(heads):
        one_kv_head(kv_head)


def attention(table, queries, grads, kv_parts, slots, first, heads):
    count = len(kv_parts)
    body = partial(attention_kernel, chips=count // 2, slots=slots, first=first, heads=heads)
    whole = pl.BlockSpec(memory_space=pltpu.VMEM)
    pairs = heads * GROUP * 3
    return pl.pallas_call(
        body,
        in_specs=[pl.BlockSpec(memory_space=pltpu.SMEM)] + [whole] * (2 + count),
        out_specs=[whole, whole],
        out_shape=[
            jax.ShapeDtypeStruct((BLOCK, heads * GROUP * HEAD_DIM), bf16),
            jax.ShapeDtypeStruct((count * BLOCK, 2 * heads * HEAD_DIM), bf16),
        ],
        scratch_shapes=[
            pltpu.VMEM((count, BLOCK, HEAD_DIM), bf16),
            pltpu.VMEM((count, HEAD_DIM, BLOCK), bf16),
            pltpu.VMEM((count, BLOCK, HEAD_DIM), bf16),
            pltpu.VMEM((count, BLOCK, HEAD_DIM), f32),
            pltpu.VMEM((count, BLOCK, HEAD_DIM), f32),
        ],
        compiler_params=pltpu.CompilerParams(vmem_limit_bytes=VMEM_ATT),
        cost_estimate=pl.CostEstimate(
            flops=pairs * 100 * BLOCK**3, bytes_accessed=4 << 20, transcendentals=pairs * BLOCK**2
        ),
        name="attention_backward",
    )(table, queries, grads, *kv_parts)

def project_kernel(mine_ref, other_ref, *refs, chips, first):
    grads_refs, out_ref, basis = refs[:-2], refs[-2], refs[-1]
    half = mine_ref.shape[0]
    core = lax.rem(lax.axis_index("seq"), 2)

    @pl.when(core == 0)
    def _():
        basis[:half] = mine_ref[...]
        basis[half:] = other_ref[...]

    @pl.when(core == 1)
    def _():
        basis[:half] = other_ref[...]
        basis[half:] = mine_ref[...]

    chosen = basis[...]
    part = grads_refs[0].shape[1] // 2
    tall = min(chips, 4) * BLOCK

    def product(start):
        rows = slice(start, start + tall)
        keys = [ref[rows, :part] for ref in grads_refs]
        values = [ref[rows, part:] for ref in grads_refs]
        return mm(jnp.concatenate(keys + values, axis=1), chosen)

    for start in range(0, chips * BLOCK, tall):
        out_ref[start : start + tall] = product(first + start).astype(out_ref.dtype)


def project(mine, other, grads, chips, first, dtype):
    rank = mine.shape[1]
    return pl.pallas_call(
        partial(project_kernel, chips=chips, first=first),
        out_shape=jax.ShapeDtypeStruct((chips * BLOCK, rank), dtype),
        scratch_shapes=[pltpu.VMEM((2 * mine.shape[0], rank), bf16)],
        compiler_params=pltpu.CompilerParams(vmem_limit_bytes=32 * 1024 * 1024),
        name="project",
    )(mine, other, *grads)


def fold_kernel(keep_ref, came_ref, own_ref, *send_refs):
    own_ref[...] = keep_ref[:BLOCK] + came_ref[:BLOCK].astype(f32)
    for index, send_ref in enumerate(send_refs):
        rows = slice((index + 1) * BLOCK, (index + 2) * BLOCK)
        send_ref[...] = (keep_ref[rows] + came_ref[rows].astype(f32)).astype(bf16)


def fold(keep, came, chips):
    rank = keep.shape[1]
    return pl.pallas_call(
        fold_kernel,
        out_shape=[jax.ShapeDtypeStruct((BLOCK, rank), f32)]
        + [jax.ShapeDtypeStruct((BLOCK, rank), bf16)] * (chips - 1),
        compiler_params=pltpu.CompilerParams(vmem_limit_bytes=32 * 1024 * 1024),
        name="fold_parts",
    )(keep, came)


def outer_kernel(x_ref, *refs, dp_count):
    p_refs, refs = refs[:dp_count], refs[dp_count:]
    keep_ref, send_ref = refs
    core = lax.rem(lax.axis_index("seq"), 2)
    me = lax.axis_index("dp")
    half = keep_ref.shape[0]
    projected = jnp.concatenate([ref[...] for ref in p_refs], axis=0)

    def product(which):
        columns = pl.ds(pl.multiple_of(which * half, half), half)
        inputs = [x_ref[jnp.bitwise_xor(me, step), :, columns] for step in range(dp_count)]
        return mm(jnp.concatenate(inputs, axis=0), projected, TN)

    send_ref[...] = product(1 - core).astype(bf16)
    keep_ref[...] = product(core)


def outer(x_all, p_parts):
    features = x_all.shape[2]
    rank = p_parts[0].shape[1]
    return pl.pallas_call(
        partial(outer_kernel, dp_count=len(p_parts)),
        out_shape=[
            jax.ShapeDtypeStruct((features // 2, rank), f32),
            jax.ShapeDtypeStruct((features // 2, rank), bf16),
        ],
        compiler_params=pltpu.CompilerParams(vmem_limit_bytes=32 * 1024 * 1024),
        name="outer_product",
    )(x_all, *p_parts)


def deal_kernel(keep_ref, came_ref, own_ref, *refs):
    send_refs, total = refs[:-1], refs[-1]
    chips = len(send_refs) + 1
    chip = lax.axis_index("seq") // 2
    share = own_ref.shape[0]
    total[...] = keep_ref[...] + came_ref[...].astype(f32)

    def rows(step):
        return pl.ds(pl.multiple_of(lax.rem(chip + step, chips) * share, share), share)

    own_ref[...] = total[rows(0)]
    for step, send_ref in enumerate(send_refs, 1):
        send_ref[...] = total[rows(step)].astype(bf16)


def deal(keep, came, chips):
    share, rank = keep.shape[0] // chips, keep.shape[1]
    return pl.pallas_call(
        deal_kernel,
        out_shape=[jax.ShapeDtypeStruct((share, rank), f32)]
        + [jax.ShapeDtypeStruct((share, rank), bf16)] * (chips - 1),
        scratch_shapes=[pltpu.VMEM(keep.shape, f32)],
        compiler_params=pltpu.CompilerParams(vmem_limit_bytes=32 * 1024 * 1024),
        name="deal_rows",
    )(keep, came)


def lay_kernel(*refs):
    part_refs, out_ref = refs[:-1], refs[-1]
    me = lax.axis_index("dp")
    share = part_refs[0].shape[0]
    for step, part_ref in enumerate(part_refs):
        at = pl.multiple_of(jnp.bitwise_xor(me, step) * share, share)
        out_ref[pl.ds(at, share)] = part_ref[...].astype(f32) * (1.0 / len(part_refs))


def lay(parts):
    share, rank = parts[0].shape
    return pl.pallas_call(
        lay_kernel,
        out_shape=jax.ShapeDtypeStruct((share * len(parts), rank), f32),
        compiler_params=pltpu.CompilerParams(vmem_limit_bytes=32 * 1024 * 1024),
        name="lay_rows",
    )(*parts)


def split_kernel(x_ref, out_ref, *, chips):
    dp_count, _, width = out_ref.shape
    share = width // (2 * chips)
    for place in range(2 * chips):
        to = (place % 2 * chips + place // 2) * share
        for group in range(dp_count):
            at = (place * dp_count + group) * share
            out_ref[group, :, to : to + share] = x_ref[:, at : at + share]


def split_input(x, chips, dp_count):
    features = x.shape[1]
    share = features // (2 * chips * dp_count)
    if share % 128 != 0:
        pieces = jnp.transpose(x.reshape(BLOCK, chips, 2, dp_count, share), (3, 0, 2, 1, 4))
        return pieces.reshape(dp_count, BLOCK, features // dp_count)
    return pl.pallas_call(
        partial(split_kernel, chips=chips),
        out_shape=jax.ShapeDtypeStruct((dp_count, BLOCK, features // dp_count), bf16),
        compiler_params=pltpu.CompilerParams(vmem_limit_bytes=16 * 1024 * 1024),
        name="split_input",
    )(x)


def local(queries, keys, values, grad_out, layer_input, basis_store, owner, layout):
    seq_count = lax.axis_size("seq")
    dp_count = lax.axis_size("dp")
    chips = seq_count // 2
    place = lax.axis_index("seq")
    chip, core = place // 2, lax.rem(place, 2)
    me = lax.axis_index("dp")
    slots = layout.shape[2]
    rank = basis_store.shape[2]

    def pair(x):
        return lax.ppermute(x, "seq", [(i, i ^ 1) for i in range(seq_count)])

    def around(x, step):
        moves = [(i, (i + 2 * step) % seq_count) for i in range(seq_count)]
        return lax.ppermute(x, "seq", moves)

    def up(x, step):
        return around(x, step)

    def down(x, step):
        return around(x, -step)

    def across(x, step):
        return lax.ppermute(x, "dp", [(i, i ^ step) for i in range(dp_count)])

    heads = KV_HEADS // CHUNKS
    part = heads * HEAD_DIM

    def packed(chunk):
        columns = slice(chunk * part, (chunk + 1) * part)
        return jnp.concatenate([keys[0][:, columns], values[0][:, columns]], axis=1)

    arrived = []
    for chunk in range(CHUNKS):
        kv = packed(chunk)
        same = [kv]
        for step in range(1, chips):
            if chunk and step == 3:
                kv, arrived[chunk - 1] = lax.optimization_barrier((kv, arrived[chunk - 1]))
            same.append(up(kv, step))
        arrived.append(same)
    beside = [pair(same[0]) for same in arrived]
    table = lists_by_length(layout, place, chips)

    pieces = KV_HEADS
    half = lax.dynamic_slice_in_dim(basis_store[0], core * pieces * HEAD_DIM, pieces * HEAD_DIM, 0)
    owners = lax.dynamic_slice_in_dim(owner, core * pieces, pieces, 0)
    from_where = (owners ^ me)[:, None, None]
    mine = half.reshape(pieces, HEAD_DIM, rank)
    step = 1
    while step < dp_count:
        came = across(mine.reshape(half.shape), step).reshape(mine.shape)
        mine = jnp.where((from_where & step) != 0, came, mine)
        step *= 2
    mine = mine.reshape(half.shape)
    other = pair(mine)

    x_pieces = split_input(layer_input[0], chips, dp_count)
    x_all = lax.all_to_all(x_pieces, "dp", 0, 0, tiled=True)

    query_grads, grads = [], []
    for chunk in range(CHUNKS):
        if chunk:
            arrived[chunk][1:], grads = lax.optimization_barrier((arrived[chunk][1:], grads))
        kv_parts = arrived[chunk] + [beside[chunk]] + [pair(piece) for piece in arrived[chunk][1:]]
        query_grad, grad = attention(
            table, queries[0], grad_out[0], kv_parts, slots, chunk * heads, heads
        )
        query_grads.append(query_grad)
        grads.append(grad)
    grad_query = jnp.concatenate(query_grads, axis=1)

    send = project(mine, other, grads, chips, chips * BLOCK, bf16)
    keep = project(mine, other, grads, chips, 0, f32)
    own, *sends = fold(keep, pair(send), chips)
    order = sorted(range(1, chips), key=lambda step: abs(2 * step - chips))
    total = own
    for step in order:
        total = total + down(sends[step - 1], step).astype(f32)
    projected = total.astype(bf16)
    p_parts = [projected] + [across(projected, step) for step in range(1, dp_count)]
    kept, sent = outer(x_all, p_parts)
    own, *sends = deal(kept, pair(sent), chips)
    total = own
    for step in order:
        total = total + around(sends[step - 1], step).astype(f32)
    rows = total.astype(bf16)
    lowrank_grad = lay([rows] + [across(rows, step) for step in range(1, dp_count)])
    return (grad_query[None], lowrank_grad)


def solution(mesh):
    in_specs = (
        P("dp", "seq", None),
        P("dp", "seq", None),
        P("dp", "seq", None),
        P("dp", "seq", None),
        P("dp", "seq", None),
        P("dp", None, None),
        P(),
        P(),
    )
    out_specs = (P("dp", "seq", None), P("seq", None))
    return jax.shard_map(local, mesh=mesh, in_specs=in_specs, out_specs=out_specs, check_vma=False)
```

```python
import math
from functools import partial

import jax
import jax.numpy as jnp
from jax import lax
from jax.experimental import pallas as pl
from jax.experimental.pallas import tpu as pltpu
from jax.sharding import PartitionSpec as P

HEADS = 32
KV_HEADS = 4
HEAD_DIM = 128
BLOCK = 128
GROUP = HEADS // KV_HEADS
UNROLL = 4
CHUNKS = 2
VMEM_ATT = 24 * 1024 * 1024
MASKED = -1e30

bf16 = jnp.bfloat16
f32 = jnp.float32
NT = (((1,), (1,)), ((), ()))
NN = (((1,), (0,)), ((), ()))
TN = (((0,), (0,)), ((), ()))


def mm(a, b, dims=NN):
    return lax.dot_general(a, b, dims, preferred_element_type=f32)


def lists_by_length(layout, place, chips):
    slots = layout.shape[2]
    chip, core = place // 2, lax.rem(place, 2)
    lists = lax.dynamic_slice_in_dim(layout, place, 1, 1)[:, 0]
    length = jnp.sum((lists >= 0).astype(jnp.int32), axis=1)
    spots = (chip - lists // 2) + chips * ((lists + core) % 2)
    earlier = jnp.arange(slots, dtype=jnp.int32)[None] < length[:, None] - 1
    spots = jnp.where(earlier, spots, 0)
    within = jnp.arange(HEADS, dtype=jnp.int32) % GROUP
    table = jnp.concatenate([within[:, None], length[:, None], spots[:, : slots - 1]], axis=1)
    table = table.reshape(KV_HEADS, GROUP, slots + 1)
    size = length.reshape(KV_HEADS, GROUP)
    inside = jnp.arange(GROUP, dtype=jnp.int32)
    mine, others = size[:, :, None], size[:, None, :]
    ahead = (others > mine) | ((others == mine) & (inside[None, None, :] < inside[None, :, None]))
    rank = jnp.sum(ahead.astype(jnp.int32), axis=2)
    chosen = rank[:, :, None] == inside[None, None, :]
    ordered = jnp.sum(jnp.where(chosen[..., None], table[:, :, None, :], 0), axis=1)
    return ordered.reshape(-1)


def attention_kernel(table_ref, q_ref, do_ref, *refs, chips, slots, first, heads):
    count = 2 * chips
    kv_refs, refs = refs[:count], refs[count:]
    dq_ref, grads_ref, kbuf, ktbuf, vbuf, dk_acc, dv_acc = refs
    row = slots + 1
    scale = HEAD_DIM ** (-0.5)
    to_exp2 = scale * math.log2(math.e)
    rows = lax.broadcasted_iota(jnp.int32, (BLOCK, BLOCK), 0)
    columns = lax.broadcasted_iota(jnp.int32, (BLOCK, BLOCK), 1)
    causal = rows <= columns

    def one_kv_head(kv_head):
        k_lane = slice(kv_head * HEAD_DIM, (kv_head + 1) * HEAD_DIM)
        v_lane = slice((heads + kv_head) * HEAD_DIM, (heads + kv_head + 1) * HEAD_DIM)
        for index in range(count):
            block = kv_refs[index][:, k_lane]
            kbuf[index] = block
            ktbuf[index] = block.T
            vbuf[index] = kv_refs[index][:, v_lane]
        dk_acc[...] = jnp.zeros_like(dk_acc)
        dv_acc[...] = jnp.zeros_like(dv_acc)

        def heads_step(step, carry):
            base = ((first + kv_head) * GROUP + step * UNROLL) * row
            most = table_ref[base + 1]

            def work(width):
                units = range(UNROLL)
                lanes_in, lanes_out, spots, valid = [], [], [], []
                for unit in units:
                    start = base + unit * row
                    head = table_ref[start]
                    length = table_ref[start + 1]
                    spots.append([0] + [table_ref[start + 1 + slot] for slot in range(1, width)])
                    valid.append([None] + [slot < length for slot in range(1, width)])
                    at_in = ((first + kv_head) * GROUP + head) * HEAD_DIM
                    at_out = (kv_head * GROUP + head) * HEAD_DIM
                    lanes_in.append(pl.ds(pl.multiple_of(at_in, HEAD_DIM), HEAD_DIM))
                    lanes_out.append(pl.ds(pl.multiple_of(at_out, HEAD_DIM), HEAD_DIM))
                qs = [q_ref[:, lanes_in[unit]] for unit in units]
                dos = [do_ref[:, lanes_in[unit]] for unit in units]
                scores, dweights = [], []
                for unit in units:
                    ks = jnp.concatenate([kbuf[spot] for spot in spots[unit]], axis=0)
                    scores.append(mm(ks, qs[unit], NT))
                for unit in units:
                    vs = jnp.concatenate([vbuf[spot] for spot in spots[unit]], axis=0)
                    dweights.append(mm(vs, dos[unit], NT))
                lows, dlows = [], []
                for unit in units:
                    pieces = []
                    for slot in range(width):
                        piece = scores[unit][slot * BLOCK : (slot + 1) * BLOCK] * to_exp2
                        shown = causal if slot == 0 else valid[unit][slot]
                        pieces.append(jnp.where(shown, piece, MASKED))
                    masked = jnp.concatenate(pieces, axis=0)
                    top = jnp.max(masked, axis=0, keepdims=True)
                    raw = jnp.exp2(masked - top)
                    weights = raw * (1.0 / jnp.sum(raw, axis=0, keepdims=True))
                    delta = jnp.sum(weights * dweights[unit], axis=0, keepdims=True)
                    lows.append(weights.astype(bf16))
                    dlows.append((weights * (dweights[unit] - delta)).astype(bf16))
                for unit in units:
                    kt = jnp.concatenate([ktbuf[spot] for spot in spots[unit]], axis=1)
                    dq_ref[:, lanes_out[unit]] = (mm(kt, dlows[unit]) * scale).astype(bf16).T
                dk_acc[0] += mm(
                    jnp.concatenate([dlow[:BLOCK] for dlow in dlows], axis=1),
                    jnp.concatenate(qs, axis=0),
                )
                dv_acc[0] += mm(
                    jnp.concatenate([low[:BLOCK] for low in lows], axis=1),
                    jnp.concatenate(dos, axis=0),
                )
                if width > 1:
                    for unit in units:
                        dk = mm(dlows[unit][BLOCK:], qs[unit])
                        dv = mm(lows[unit][BLOCK:], dos[unit])
                        for slot in range(1, width):
                            part = slice((slot - 1) * BLOCK, slot * BLOCK)
                            dk_acc[spots[unit][slot]] += dk[part]
                            dv_acc[spots[unit][slot]] += dv[part]

            for width in range(1, slots + 1):
                pl.when(most == width)(partial(work, width))
            return carry

        lax.fori_loop(0, GROUP // UNROLL, heads_step, 0)
        for index in range(count):
            at = slice(index * BLOCK, (index + 1) * BLOCK)
            grads_ref[at, k_lane] = (dk_acc[index] * scale).astype(bf16)
            grads_ref[at, v_lane] = dv_acc[index].astype(bf16)

    for kv_head in range(heads):
        one_kv_head(kv_head)


def attention(table, queries, grads, kv_parts, slots, first, heads):
    count = len(kv_parts)
    body = partial(attention_kernel, chips=count // 2, slots=slots, first=first, heads=heads)
    whole = pl.BlockSpec(memory_space=pltpu.VMEM)
    pairs = heads * GROUP * 3
    return pl.pallas_call(
        body,
        in_specs=[pl.BlockSpec(memory_space=pltpu.SMEM)] + [whole] * (2 + count),
        out_specs=[whole, whole],
        out_shape=[
            jax.ShapeDtypeStruct((BLOCK, heads * GROUP * HEAD_DIM), bf16),
            jax.ShapeDtypeStruct((count * BLOCK, 2 * heads * HEAD_DIM), bf16),
        ],
        scratch_shapes=[
            pltpu.VMEM((count, BLOCK, HEAD_DIM), bf16),
            pltpu.VMEM((count, HEAD_DIM, BLOCK), bf16),
            pltpu.VMEM((count, BLOCK, HEAD_DIM), bf16),
            pltpu.VMEM((count, BLOCK, HEAD_DIM), f32),
            pltpu.VMEM((count, BLOCK, HEAD_DIM), f32),
        ],
        compiler_params=pltpu.CompilerParams(vmem_limit_bytes=VMEM_ATT),
        cost_estimate=pl.CostEstimate(
            flops=pairs * 100 * BLOCK**3, bytes_accessed=4 << 20, transcendentals=pairs * BLOCK**2
        ),
        name="attention_backward",
    )(table, queries, grads, *kv_parts)

def project_kernel(mine_ref, other_ref, *refs, chips, first):
    grads_refs, out_ref, basis = refs[:-2], refs[-2], refs[-1]
    half = mine_ref.shape[0]
    core = lax.rem(lax.axis_index("seq"), 2)

    @pl.when(core == 0)
    def _():
        basis[:half] = mine_ref[...]
        basis[half:] = other_ref[...]

    @pl.when(core == 1)
    def _():
        basis[:half] = other_ref[...]
        basis[half:] = mine_ref[...]

    chosen = basis[...]
    part = grads_refs[0].shape[1] // 2
    tall = min(chips, 4) * BLOCK

    def product(start):
        rows = slice(start, start + tall)
        keys = [ref[rows, :part] for ref in grads_refs]
        values = [ref[rows, part:] for ref in grads_refs]
        return mm(jnp.concatenate(keys + values, axis=1), chosen)

    for start in range(0, chips * BLOCK, tall):
        out_ref[start : start + tall] = product(first + start).astype(out_ref.dtype)


def project(mine, other, grads, chips, first, dtype):
    rank = mine.shape[1]
    return pl.pallas_call(
        partial(project_kernel, chips=chips, first=first),
        out_shape=jax.ShapeDtypeStruct((chips * BLOCK, rank), dtype),
        scratch_shapes=[pltpu.VMEM((2 * mine.shape[0], rank), bf16)],
        compiler_params=pltpu.CompilerParams(vmem_limit_bytes=32 * 1024 * 1024),
        name="project",
    )(mine, other, *grads)


def fold_kernel(keep_ref, came_ref, own_ref, *send_refs):
    own_ref[...] = keep_ref[:BLOCK] + came_ref[:BLOCK].astype(f32)
    for index, send_ref in enumerate(send_refs):
        rows = slice((index + 1) * BLOCK, (index + 2) * BLOCK)
        send_ref[...] = (keep_ref[rows] + came_ref[rows].astype(f32)).astype(bf16)


def fold(keep, came, chips):
    rank = keep.shape[1]
    return pl.pallas_call(
        fold_kernel,
        out_shape=[jax.ShapeDtypeStruct((BLOCK, rank), f32)]
        + [jax.ShapeDtypeStruct((BLOCK, rank), bf16)] * (chips - 1),
        compiler_params=pltpu.CompilerParams(vmem_limit_bytes=32 * 1024 * 1024),
        name="fold_parts",
    )(keep, came)


def outer_kernel(x_ref, *refs, dp_count):
    p_refs, refs = refs[:dp_count], refs[dp_count:]
    keep_ref, send_ref = refs
    core = lax.rem(lax.axis_index("seq"), 2)
    me = lax.axis_index("dp")
    half = keep_ref.shape[0]
    projected = jnp.concatenate([ref[...] for ref in p_refs], axis=0)

    def product(which):
        columns = pl.ds(pl.multiple_of(which * half, half), half)
        inputs = [x_ref[jnp.bitwise_xor(me, step), :, columns] for step in range(dp_count)]
        return mm(jnp.concatenate(inputs, axis=0), projected, TN)

    send_ref[...] = product(1 - core).astype(bf16)
    keep_ref[...] = product(core)


def outer(x_all, p_parts):
    features = x_all.shape[2]
    rank = p_parts[0].shape[1]
    return pl.pallas_call(
        partial(outer_kernel, dp_count=len(p_parts)),
        out_shape=[
            jax.ShapeDtypeStruct((features // 2, rank), f32),
            jax.ShapeDtypeStruct((features // 2, rank), bf16),
        ],
        compiler_params=pltpu.CompilerParams(vmem_limit_bytes=32 * 1024 * 1024),
        name="outer_product",
    )(x_all, *p_parts)


def deal_kernel(keep_ref, came_ref, own_ref, *refs):
    send_refs, total = refs[:-1], refs[-1]
    chips = len(send_refs) + 1
    chip = lax.axis_index("seq") // 2
    share = own_ref.shape[0]
    total[...] = keep_ref[...] + came_ref[...].astype(f32)

    def rows(step):
        return pl.ds(pl.multiple_of(lax.rem(chip + step, chips) * share, share), share)

    own_ref[...] = total[rows(0)]
    for step, send_ref in enumerate(send_refs, 1):
        send_ref[...] = total[rows(step)].astype(bf16)


def deal(keep, came, chips):
    share, rank = keep.shape[0] // chips, keep.shape[1]
    return pl.pallas_call(
        deal_kernel,
        out_shape=[jax.ShapeDtypeStruct((share, rank), f32)]
        + [jax.ShapeDtypeStruct((share, rank), bf16)] * (chips - 1),
        scratch_shapes=[pltpu.VMEM(keep.shape, f32)],
        compiler_params=pltpu.CompilerParams(vmem_limit_bytes=32 * 1024 * 1024),
        name="deal_rows",
    )(keep, came)


def lay_kernel(*refs):
    part_refs, out_ref = refs[:-1], refs[-1]
    me = lax.axis_index("dp")
    share = part_refs[0].shape[0]
    for step, part_ref in enumerate(part_refs):
        at = pl.multiple_of(jnp.bitwise_xor(me, step) * share, share)
        out_ref[pl.ds(at, share)] = part_ref[...].astype(f32) * (1.0 / len(part_refs))


def lay(parts):
    share, rank = parts[0].shape
    return pl.pallas_call(
        lay_kernel,
        out_shape=jax.ShapeDtypeStruct((share * len(parts), rank), f32),
        compiler_params=pltpu.CompilerParams(vmem_limit_bytes=32 * 1024 * 1024),
        name="lay_rows",
    )(*parts)


def split_kernel(x_ref, out_ref, *, chips):
    dp_count, _, width = out_ref.shape
    share = width // (2 * chips)
    for place in range(2 * chips):
        to = (place % 2 * chips + place // 2) * share
        for group in range(dp_count):
            at = (place * dp_count + group) * share
            out_ref[group, :, to : to + share] = x_ref[:, at : at + share]


def split_input(x, chips, dp_count):
    features = x.shape[1]
    share = features // (2 * chips * dp_count)
    if share % 128 != 0:
        pieces = jnp.transpose(x.reshape(BLOCK, chips, 2, dp_count, share), (3, 0, 2, 1, 4))
        return pieces.reshape(dp_count, BLOCK, features // dp_count)
    return pl.pallas_call(
        partial(split_kernel, chips=chips),
        out_shape=jax.ShapeDtypeStruct((dp_count, BLOCK, features // dp_count), bf16),
        compiler_params=pltpu.CompilerParams(vmem_limit_bytes=16 * 1024 * 1024),
        name="split_input",
    )(x)


def local(queries, keys, values, grad_out, layer_input, basis_store, owner, layout):
    seq_count = lax.axis_size("seq")
    dp_count = lax.axis_size("dp")
    chips = seq_count // 2
    place = lax.axis_index("seq")
    chip, core = place // 2, lax.rem(place, 2)
    me = lax.axis_index("dp")
    slots = layout.shape[2]
    rank = basis_store.shape[2]

    def pair(x):
        return lax.ppermute(x, "seq", [(i, i ^ 1) for i in range(seq_count)])

    def around(x, step):
        moves = [(i, (i + 2 * step) % seq_count) for i in range(seq_count)]
        return lax.ppermute(x, "seq", moves)

    def up(x, step):
        return around(x, step)

    def down(x, step):
        return around(x, -step)

    def across(x, step):
        return lax.ppermute(x, "dp", [(i, i ^ step) for i in range(dp_count)])

    heads = KV_HEADS // CHUNKS
    part = heads * HEAD_DIM

    def packed(chunk):
        columns = slice(chunk * part, (chunk + 1) * part)
        return jnp.concatenate([keys[0][:, columns], values[0][:, columns]], axis=1)

    arrived = []
    for chunk in range(CHUNKS):
        kv = packed(chunk)
        same = [kv]
        for step in range(1, chips):
            if chunk and step == 3:
                kv, arrived[chunk - 1] = lax.optimization_barrier((kv, arrived[chunk - 1]))
            same.append(up(kv, step))
        arrived.append(same)
    beside = [pair(same[0]) for same in arrived]
    table = lists_by_length(layout, place, chips)

    pieces = KV_HEADS
    half = lax.dynamic_slice_in_dim(basis_store[0], core * pieces * HEAD_DIM, pieces * HEAD_DIM, 0)
    owners = lax.dynamic_slice_in_dim(owner, core * pieces, pieces, 0)
    from_where = (owners ^ me)[:, None, None]
    mine = half.reshape(pieces, HEAD_DIM, rank)
    step = 1
    while step < dp_count:
        came = across(mine.reshape(half.shape), step).reshape(mine.shape)
        mine = jnp.where((from_where & step) != 0, came, mine)
        step *= 2
    mine = mine.reshape(half.shape)
    other = pair(mine)

    x_pieces = split_input(layer_input[0], chips, dp_count)
    x_all = lax.all_to_all(x_pieces, "dp", 0, 0, tiled=True)

    query_grads, grads = [], []
    for chunk in range(CHUNKS):
        if chunk:
            arrived[chunk][1:], grads = lax.optimization_barrier((arrived[chunk][1:], grads))
        kv_parts = arrived[chunk] + [beside[chunk]] + [pair(piece) for piece in arrived[chunk][1:]]
        query_grad, grad = attention(
            table, queries[0], grad_out[0], kv_parts, slots, chunk * heads, heads
        )
        query_grads.append(query_grad)
        grads.append(grad)
    grad_query = jnp.concatenate(query_grads, axis=1)

    send = project(mine, other, grads, chips, chips * BLOCK, bf16)
    keep = project(mine, other, grads, chips, 0, f32)
    own, *sends = fold(keep, pair(send), chips)
    order = sorted(range(1, chips), key=lambda step: abs(2 * step - chips))
    total = own
    for step in order:
        total = total + down(sends[step - 1], step).astype(f32)
    projected = total.astype(bf16)
    moved = {step: across(projected, step) for step in reversed(range(1, dp_count))}
    p_parts = [projected] + [moved[step] for step in range(1, dp_count)]
    kept, sent = outer(x_all, p_parts)
    own, *sends = deal(kept, pair(sent), chips)
    total = own
    for step in order:
        total = total + around(sends[step - 1], step).astype(f32)
    rows = total.astype(bf16)
    moved = {step: across(rows, step) for step in reversed(range(1, dp_count))}
    lowrank_grad = lay([rows] + [moved[step] for step in range(1, dp_count)])
    return (grad_query[None], lowrank_grad)


def solution(mesh):
    in_specs = (
        P("dp", "seq", None),
        P("dp", "seq", None),
        P("dp", "seq", None),
        P("dp", "seq", None),
        P("dp", "seq", None),
        P("dp", None, None),
        P(),
        P(),
    )
    out_specs = (P("dp", "seq", None), P("seq", None))
    return jax.shard_map(local, mesh=mesh, in_specs=in_specs, out_specs=out_specs, check_vma=False)
```
